512 devices in a mesh: depth: 64 (over z, x), batch: 8 (over y, core).
Axes of the slice: x: 4, y: 4, z: 16, core: 2. Of those that a mesh axis runs over, the one named last changes fastest.
Arguments:
- inputs: float32 [16, 64, 512], P('batch'), parts along dimension 0, may hold values from -6 to 6
- attn_in: bfloat16 [64, 512, 1536], P('depth'), may hold values from -0.25 to 0.25
- attn_out: bfloat16 [64, 512, 512], P('depth'), may hold values from -0.25 to 0.25
- mlp_in: bfloat16 [64, 512, 1024], P('depth'), may hold values from -0.25 to 0.25
- mlp_out: bfloat16 [64, 1024, 512], P('depth'), may hold values from -0.1875 to 0.1875
- norm_gain: float32 [64, 512], P('depth'), may hold values from 0.25 to 1.75
- head_gain: float32 [64, 64], P('depth'), may hold values from 0.25 to 1.75
Outputs:
- states: float32 [64, 16, 64, 512], P('depth', 'batch'), parts along dimension 1
- coarse_points: float32 [64, 16, 64, 512], P('depth', 'batch'), parts along dimension 1
The draws below stay inside these ranges and needn't reach their ends.
There are 8 independent parts, one for each index of `batch`. The reference program is written for one: setup_inputs(seed, part) draws one part's arguments, and reference() takes and returns one part's arrays. A program takes and returns all parts, laid end to end along the dimension named above; an argument that names none is the same for every part. Nothing has to cross between parts.
All inputs are finite; a program needn't handle non-finite values.
Results may differ from the reference program's by a relative error of at most 0.014.
Values sent between devices are 32-bit elements; how exact they have to be, the bound alone decides.
No kernel may reach another device: no remote copies, remote signals or barrier semaphores. Data moves between devices by JAX's collectives and lax.ppermute only.
A program may use at most 64 MiB of HBM per device.

```python
import math
import jax
import jax.numpy as jnp
from jax import lax

D = 512
HEAD_DIM = 64
FF = 1024
FRAMES = 64
MICRO = 2
COARSEN = 4
LAYERS = 64


def steps_of(own_key, extent, pieces, least, high):
    def one(position, parts):
        heights = jax.random.uniform(jax.random.fold_in(jax.random.fold_in(own_key, 6), position), (parts,), jnp.float32, least / len(pieces), high / len(pieces))
        return jnp.repeat(jnp.exp(heights), extent[position] // parts).reshape((-1,) + (1,) * (len(extent) - position - 1))

    gain = one(*pieces[0])
    for cut in pieces[1:]:
        gain = gain * one(*cut)
    return gain


def noise(stream_key, extent, width, bound, split=(), kind=jnp.bfloat16):
    array = width * jax.random.normal(stream_key, extent, jnp.float32)
    if split:
        array = array * steps_of(stream_key, extent, split, -0.22, 0.18)
    return jnp.clip(array, -bound, bound).astype(kind)


def setup_inputs(seed: int = 0, part: int = 0) -> dict:
    streams_of = jax.random.split(jax.random.key(seed), 8)
    part_splits = jax.random.split(jax.random.fold_in(streams_of[7], part), 8)
    inputs = noise(part_splits[0], (MICRO, FRAMES, D), 1.0, 6.0, (), jnp.float32)
    attn_in = noise(streams_of[1], (LAYERS, D, 3 * D), D ** -0.5, 0.25, ((0, 64),))
    attn_out = noise(streams_of[2], (LAYERS, D, D), D ** -0.5, 0.25, ((0, 64),))
    mlp_in = noise(streams_of[3], (LAYERS, D, FF), D ** -0.5, 0.25, ((0, 64),))
    mlp_out = noise(streams_of[4], (LAYERS, FF, D), FF ** -0.5, 0.1875, ((0, 64),))
    norm_gain = jnp.clip(1.0 + 0.15 * jax.random.normal(streams_of[5], (LAYERS, D), jnp.float32), 0.25, 1.75)
    head_gain = jnp.clip(1.0 + 0.15 * jax.random.normal(streams_of[6], (LAYERS, HEAD_DIM), jnp.float32), 0.25, 1.75)
    return {"inputs": inputs, "attn_in": attn_in, "attn_out": attn_out, "mlp_in": mlp_in, "mlp_out": mlp_out, "norm_gain": norm_gain, "head_gain": head_gain}


step_size = 0.25
epsilon = 1e-06

def normalize(values):
    return values * lax.rsqrt(lax.optimization_barrier(jnp.mean(values * values, axis=-1, keepdims=True)) + epsilon)

def layer_delta(current, w_qkv, w_out, w_up, w_down, in_gain, qk_gain):
    batch_size, frame_count, model_width = current.shape
    head_dim = qk_gain.shape[0]
    head_count = model_width // head_dim
    normed = (normalize(current) * in_gain).astype(jnp.bfloat16)
    projected = jnp.dot(normed, w_qkv, preferred_element_type=jnp.float32)
    projected = projected.reshape(batch_size, frame_count, 3, head_count, head_dim)
    query_rows = (normalize(projected[:, :, 0]) * qk_gain).astype(jnp.bfloat16)
    key_rows = (normalize(projected[:, :, 1]) * qk_gain).astype(jnp.bfloat16)
    value_rows = projected[:, :, 2].astype(jnp.bfloat16)
    scores = jnp.einsum('bqhe,bkhe->bhqk', query_rows.astype(jnp.float32), key_rows.astype(jnp.float32)) / math.sqrt(head_dim)
    causal = jnp.arange(frame_count)[:, None] >= jnp.arange(frame_count)[None, :]
    exp_scores = jnp.where(causal, jnp.exp(scores), 0.0)
    probs = (exp_scores / lax.optimization_barrier(jnp.sum(exp_scores, axis=-1, keepdims=True))).astype(jnp.bfloat16)
    context = jnp.einsum('bhqk,bkhe->bqhe', probs.astype(jnp.float32), value_rows.astype(jnp.float32))
    context = context.astype(jnp.bfloat16).reshape(batch_size, frame_count, model_width)
    attention = jnp.dot(context, w_out, preferred_element_type=jnp.float32)
    hidden = jax.nn.gelu(jnp.dot(normed, w_up, preferred_element_type=jnp.float32), approximate=True).astype(jnp.bfloat16)
    return attention + jnp.dot(hidden, w_down, preferred_element_type=jnp.float32)

def reference(inputs, attn_in, attn_out, mlp_in, mlp_out, norm_gain, head_gain):
    blocks = LAYERS // COARSEN
    stacked = (attn_in, attn_out, mlp_in, mlp_out, norm_gain, head_gain)
    grouped = tuple((item.reshape((blocks, COARSEN) + item.shape[1:]) for item in stacked))

    def slot_weights(slot):
        return tuple((item[:, slot] for item in grouped))
    apply_all = jax.vmap(layer_delta)
    apply_shared = jax.vmap(layer_delta, in_axes=(None, 0, 0, 0, 0, 0, 0))
    repeated = jnp.broadcast_to(inputs, (blocks,) + inputs.shape)
    moving = repeated
    base_sum = jnp.zeros_like(repeated)
    for slot in range(COARSEN):
        if slot == 0:
            change = apply_all(repeated, *slot_weights(0))
            base_sum = base_sum + change
        else:
            base_sum = base_sum + apply_all(repeated, *slot_weights(slot))
            change = apply_all(moving, *slot_weights(slot))
        moving = moving + step_size * change
    offsets = moving - repeated - step_size * base_sum

    def coarse_turn(current, item):
        offset, weights = item
        increments = apply_shared(current, *weights)
        following = offset + current + step_size * lax.optimization_barrier(jnp.sum(increments, axis=0))
        return (following, following)
    later = lax.scan(coarse_turn, inputs, (offsets, grouped))[1]
    starts = jnp.concatenate([inputs[None], later[:-1]], axis=0)
    moving = starts
    for slot in range(COARSEN):
        moving = moving + step_size * apply_all(moving, *slot_weights(slot))
    fresh = moving
    moving = jnp.concatenate([inputs[None], fresh[:-1]], axis=0)
    finals = []
    for slot in range(COARSEN - 1):
        moving = moving + step_size * apply_all(moving, *slot_weights(slot))
        finals.append(moving)
    result = jnp.stack(finals + [fresh], axis=1).reshape((LAYERS,) + inputs.shape)
    coarse_points = jnp.repeat(later, COARSEN, axis=0)
    return (result, coarse_points)
```

```python
import jax
import jax.numpy as jnp
from jax import lax
from jax.experimental import pallas as pl
from jax.experimental.pallas import tpu as pltpu
from jax.sharding import PartitionSpec as P

F32, BF16 = jnp.float32, jnp.bfloat16
COARSEN = 4
STEP = 0.25
EPS = 1e-6
FRAMES, WIDTH, HEAD = 64, 512, 64
ROWS = 4096
CHUNKS = 2
QUAD = 4 * HEAD
VMEM_SPEC = pl.BlockSpec(memory_space=pltpu.VMEM)
SMEM_SPEC = pl.BlockSpec(memory_space=pltpu.SMEM)
ANY_SPEC = pl.BlockSpec(memory_space=pl.ANY)


def dot(left, right):
    return jnp.dot(left, right, preferred_element_type=F32)


def delta(v, w, gains, layer):
    norm_gain = gains[pl.ds(layer * 8, 1), :]
    head_gain = gains[pl.ds(layer * 8 + 1, 1), :QUAD]
    row = lax.broadcasted_iota(jnp.int32, (FRAMES, QUAD), 0)
    lane = lax.broadcasted_iota(jnp.int32, (FRAMES, QUAD), 1)
    causal = row >= lane % HEAD
    masks = [jnp.where(lane // HEAD == h, 1.0, 0.0).astype(BF16) for h in range(4)]
    ones = jnp.where(
        lax.broadcasted_iota(jnp.int32, (QUAD, QUAD), 0) // HEAD
        == lax.broadcasted_iota(jnp.int32, (QUAD, QUAD), 1) // HEAD,
        1.0,
        0.0,
    ).astype(BF16)

    def block(i):
        return w[layer, i * WIDTH : (i + 1) * WIDTH, :]

    scale = lax.rsqrt(jnp.mean(v * v, axis=-1, keepdims=True) + EPS)
    normed = (v * scale * norm_gain).astype(BF16)
    q, k = dot(normed, block(0)), dot(normed, block(1))
    parts = [q[:, :QUAD], q[:, QUAD:], k[:, :QUAD], k[:, QUAD:]]
    stacked = jnp.concatenate(parts, axis=0)
    squares = dot((stacked * stacked).astype(BF16), ones) * (1.0 / HEAD)
    unit = stacked * lax.rsqrt(squares + EPS) * head_gain
    value = dot(normed, block(2)).astype(BF16)
    exps, values = [], []
    for g in range(2):
        qg = (unit[g * FRAMES : (g + 1) * FRAMES] * (HEAD**-0.5)).astype(BF16)
        kg = unit[(2 + g) * FRAMES : (3 + g) * FRAMES].astype(BF16)
        vg = value[:, g * QUAD : (g + 1) * QUAD]
        keys = jnp.concatenate([kg * m for m in masks], axis=0)
        values.append(jnp.concatenate([vg * m for m in masks], axis=0))
        scores = lax.dot_general(qg, keys, (((1,), (1,)), ((), ())), preferred_element_type=F32)
        exps.append(jnp.where(causal, jnp.exp(scores), 0.0).astype(BF16))
    sums = dot(jnp.concatenate(exps, axis=0), ones)
    context = jnp.concatenate(
        [dot(exps[g], values[g]) / sums[g * FRAMES : (g + 1) * FRAMES] for g in range(2)], axis=1
    ).astype(BF16)
    total = dot(context, block(3))
    for half in range(2):
        up = dot(normed, block(4 + half))
        inner = 0.7978845608028654 * (up + 0.044715 * (up * up * up))
        hidden = (0.5 * up * (1.0 + jnp.tanh(inner))).astype(BF16)
        total = total + dot(hidden, block(6 + half))
    return total


def first_body(place, v, gains, w, base, moved):
    start = v[...]
    change = delta(start, w, gains, 0)
    base[...] = STEP * (change + delta(start, w, gains, 1))
    after = start + STEP * change
    moved[...] = after + STEP * delta(after, w, gains, 1)


def chain_body(low, high, half, count, place, v, gains, w, *outs):
    @pl.when((place[0] >= low) & (place[0] <= high) & (place[2] == half))
    def _():
        state = v[...]
        for i in range(count):
            state = state + STEP * delta(state, w, gains, i)
            outs[i][...] = state


def coarse_body(turn, place, near, far, offset, gains, w, term, state):
    @pl.when(place[0] == turn)
    def _():
        value = near[...] + far[...]
        state[...] = value
        held = jnp.where(place[2] == 0, 1.0, 0.0).astype(F32)
        term[...] = (
            held * value
            + offset[...]
            + STEP * (delta(value, w, gains, 0) + delta(value, w, gains, 1))
        )


PARAMS = pltpu.CompilerParams(vmem_limit_bytes=24 * 2**20)
STATE = jax.ShapeDtypeStruct((FRAMES, WIDTH), F32)


def run(body, name, count, place, *arrays):
    return pl.pallas_call(
        body,
        out_shape=[STATE] * count,
        in_specs=[SMEM_SPEC] + [VMEM_SPEC] * len(arrays),
        out_specs=[VMEM_SPEC] * count,
        compiler_params=PARAMS,
        name=name,
    )(place, *arrays)


def first(place, v, gains, w):
    return run(first_body, "first", 2, place, v, gains, w)


def chain(low, high, half, count, place, v, gains, w):
    def body(*refs):
        chain_body(low, high, half, count, *refs)

    return run(body, "chain", count, place, v, gains, w)


def coarse(turn, place, near, far, offset, gains, w):
    def body(*refs):
        coarse_body(turn, *refs)

    return run(body, "coarse", 2, place, near, far, offset, gains, w)


def load_body(place, attn_in, attn_out, mlp_in, mlp_out, *rest):
    pieces, (w, buffer, own_sem, sem) = rest[:-4], rest[-4:]
    piece_rows = ROWS // (4 * CHUNKS)
    slot = place[1] % 2
    own = []
    for i in range(3):
        own.append((attn_in.at[0, :, pl.ds(i * WIDTH, WIDTH)], i * WIDTH, WIDTH))
    own.append((attn_out.at[0], 3 * WIDTH, WIDTH))
    for i in range(2):
        own.append((mlp_in.at[0, :, pl.ds(i * WIDTH, WIDTH)], (4 + i) * WIDTH, WIDTH))
    own.append((mlp_out.at[0], 6 * WIDTH, 2 * WIDTH))
    copies = [
        pltpu.make_async_copy(src, w.at[slot, pl.ds(at, n), :], own_sem.at[i])
        for i, (src, at, n) in enumerate(own)
    ]
    for copy in copies:
        copy.start()
    parity, core = place[3], place[4]
    half = piece_rows // 2
    todo = []
    for j in range(CHUNKS):
        direct, lower, upper, swapped = pieces[4 * j : 4 * j + 4]
        base = j * 4 * piece_rows
        here = base + (parity * 2 + core) * piece_rows
        beside = base + ((1 - parity) * 2 + core) * piece_rows
        other = base + (parity * 2 + 1 - core) * piece_rows
        cross = base + ((1 - parity) * 2 + 1 - core) * piece_rows
        todo += [
            (direct.at[pl.ds(0, half)], here),
            (direct.at[pl.ds(half, half)], here + half),
            (lower, beside),
            (upper, beside + half),
            (swapped.at[pl.ds(0, half)], other),
            (swapped.at[pl.ds(half, half)], other + half),
            (swapped.at[pl.ds(2 * half, half)], cross),
            (swapped.at[pl.ds(3 * half, half)], cross + half),
        ]

    def fetch(i):
        return pltpu.make_async_copy(todo[i][0], buffer.at[i % 3], sem.at[i % 3])

    fetch(0).start()
    fetch(1).start()
    for i in range(len(todo)):
        if i + 2 < len(todo):
            fetch(i + 2).start()
        fetch(i).wait()
        at = pl.multiple_of(todo[i][1], half)
        w[1 - slot, pl.ds(at, half), :] = buffer[i % 3].astype(BF16)
    for copy in copies:
        copy.wait()


def load(place, weights, pieces):
    half = ROWS // (8 * CHUNKS)
    return pl.pallas_call(
        load_body,
        out_shape=pltpu.VMEM((2, ROWS, WIDTH), BF16),
        in_specs=[SMEM_SPEC] + [ANY_SPEC] * (4 + len(pieces)),
        out_specs=VMEM_SPEC,
        scratch_shapes=[
            pltpu.VMEM((3, half, WIDTH), F32),
            pltpu.SemaphoreType.DMA((7,)),
            pltpu.SemaphoreType.DMA((3,)),
        ],
        compiler_params=pltpu.CompilerParams(vmem_limit_bytes=8 * 2**20),
        name="load",
    )(place, *weights, *pieces)


def on_device(inputs, attn_in, attn_out, mlp_in, mlp_out, norm_gain, head_gain):
    layers, groups = lax.axis_size("depth"), lax.axis_size("batch")
    blocks = layers // COARSEN
    device, group = lax.axis_index("depth"), lax.axis_index("batch")
    z, x = device // COARSEN, device % COARSEN
    odd, half = x % 2, x // 2
    row, core = group // 2, group % 2
    parity = row % 2
    place = jnp.stack([z, x, half, parity, core]).astype(jnp.int32)

    def move(array, pairs):
        return lax.ppermute(array, "depth", pairs)

    def within(array, source, by, low=0, high=blocks - 1):
        pairs = [
            (COARSEN * k + i, COARSEN * k + (i ^ by)) for k in range(low, high + 1) for i in source
        ]
        return move(array, pairs)

    own = jnp.concatenate(
        [attn_in[0, :, i * WIDTH : (i + 1) * WIDTH] for i in range(3)]
        + [attn_out[0]]
        + [mlp_in[0, :, i * WIDTH : (i + 1) * WIDTH] for i in range(2)]
        + [mlp_out[0]],
        axis=0,
    )
    own_gains = jnp.concatenate(
        [norm_gain, jnp.tile(head_gain, (1, WIDTH // HEAD)), jnp.zeros((6, WIDTH), F32)], axis=0
    )
    piece_rows = ROWS // (4 * CHUNKS)
    half_rows = piece_rows // 2
    rows = groups // 2
    onward = [(2 * r + c, 2 * ((r + 1) % rows) + c) for r in range(rows) for c in range(2)]
    back = [(2 * r + c, 2 * ((r - 1) % rows) + c) for r in range(rows) for c in range(2)]
    swap = [(g, g ^ 1) for g in range(groups)]
    pieces = []
    for j in range(CHUNKS):
        at = j * 4 * piece_rows + (parity * 2 + core) * piece_rows
        piece = lax.dynamic_slice(own, (at, 0), (piece_rows, WIDTH)).astype(F32)
        if j == 0:
            piece = jnp.concatenate([piece, own_gains], axis=0)
        direct = within(piece, range(COARSEN), 1)
        if j == 0:
            partner_gains = direct[piece_rows:]
            direct = direct[:piece_rows]
        lower = lax.ppermute(direct[:half_rows], "batch", onward)
        upper = lax.ppermute(direct[half_rows:], "batch", back)
        swapped = lax.ppermute(jnp.concatenate([direct, lower, upper], axis=0), "batch", swap)
        pieces += [direct, lower, upper, swapped]
    w = load(place, (attn_in, attn_out, mlp_in, mlp_out), pieces)
    gains = jnp.where(
        odd == 0,
        jnp.concatenate([own_gains, partner_gains], axis=0),
        jnp.concatenate([partner_gains, own_gains], axis=0),
    )

    start = jnp.where(odd == 0, inputs[0], inputs[1])
    last = blocks - 1
    front, rear = (0, 1), (2, 3)

    base, moved = first(place, start, gains, w)
    moved = within(moved, front, 2)
    _, ended = chain(0, last, 1, 2, place, moved, gains, w)
    offset = jnp.where(half == 1, ended - start, 0.0) - base
    term = jnp.where(half == 1, ended, 0.0)
    state = start
    kept = term
    for turn in range(1, blocks):
        pairs = [COARSEN * (turn - 1) + i for i in range(COARSEN)]
        near = move(term, [(p, p + COARSEN) for p in pairs])
        far = move(term, [(p, (p ^ 2) + COARSEN) for p in pairs])
        term, value = coarse(turn, place, near, far, offset, gains, w)
        kept = jnp.where(z == turn, term, kept)
        state = jnp.where(z == turn, value, state)
        if turn == last - 1:
            early = state

    def relax(low, high, value):
        _, middle = chain(low, high, 0, 2, place, value, gains, w)
        middle = within(middle, front, 2, low, high)
        return chain(low, high, 1, 2, place, middle, gains, w)[1]

    fresh = relax(0, last - 1, early)
    handed = move(
        fresh, [(COARSEN * k + i, COARSEN * (k + 1) + (i ^ 2)) for k in range(last) for i in rear]
    )
    fresh = jnp.where(z == last, relax(last, last, state), fresh)
    restart = jnp.where(z == 0, start, handed)
    state_0, state_1 = chain(0, last, 0, 2, place, restart, gains, w)
    (state_2,) = chain(0, last, 1, 1, place, within(state_1, front, 2), gains, w)

    def both(mine, send):
        got = within(send, range(COARSEN), 1)
        return jnp.where(odd == 0, jnp.stack([mine, got]), jnp.stack([got, mine]))

    corrected = kept + within(kept, range(COARSEN), 2)
    ahead = both(corrected, corrected)
    lower = jnp.where(half == 0, state_0, state_2)
    upper = jnp.where(half == 0, state_1, fresh)
    output = both(jnp.where(odd == 0, lower, upper), jnp.where(odd == 0, upper, lower))
    return (output[None], ahead[None])


def solution(mesh):
    in_specs = (
        P("batch", None, None),
        P("depth", None, None),
        P("depth", None, None),
        P("depth", None, None),
        P("depth", None, None),
        P("depth", None),
        P("depth", None),
    )
    out_specs = (P("depth", "batch", None, None), P("depth", "batch", None, None))
    return jax.shard_map(
        on_device, mesh=mesh, in_specs=in_specs, out_specs=out_specs, check_vma=False
    )
```

```python
import jax
import jax.numpy as jnp
from jax import lax
from jax.experimental import pallas as pl
from jax.experimental.pallas import tpu as pltpu
from jax.sharding import PartitionSpec as P

F32, BF16 = jnp.float32, jnp.bfloat16
COARSEN = 4
STEP = 0.25
EPS = 1e-6
FRAMES, WIDTH, HEAD = 64, 512, 64
ROWS = 4096
CHUNKS = 4
QUAD = 4 * HEAD
VMEM_SPEC = pl.BlockSpec(memory_space=pltpu.VMEM)
SMEM_SPEC = pl.BlockSpec(memory_space=pltpu.SMEM)
HBM_SPEC = pl.BlockSpec(memory_space=pltpu.HBM)


def dot(left, right):
    return jnp.dot(left, right, preferred_element_type=F32)


def delta(v, w, gains, place, layer):
    at = (place[1] % 2 + layer) % 2 * 8
    norm_gain = gains[pl.ds(at, 1), :]
    head_gain = gains[pl.ds(at + 1, 1), :QUAD]
    row = lax.broadcasted_iota(jnp.int32, (FRAMES, QUAD), 0)
    lane = lax.broadcasted_iota(jnp.int32, (FRAMES, QUAD), 1)
    causal = row >= lane % HEAD
    masks = [jnp.where(lane // HEAD == h, 1.0, 0.0).astype(BF16) for h in range(4)]
    ones = jnp.where(
        lax.broadcasted_iota(jnp.int32, (QUAD, QUAD), 0) // HEAD
        == lax.broadcasted_iota(jnp.int32, (QUAD, QUAD), 1) // HEAD,
        1.0,
        0.0,
    ).astype(BF16)

    def block(i):
        return w[layer, i * WIDTH : (i + 1) * WIDTH, :]

    scale = lax.rsqrt(jnp.mean(v * v, axis=-1, keepdims=True) + EPS)
    normed = (v * scale * norm_gain).astype(BF16)
    q, k = dot(normed, block(0)), dot(normed, block(1))
    parts = [q[:, :QUAD], q[:, QUAD:], k[:, :QUAD], k[:, QUAD:]]
    stacked = jnp.concatenate(parts, axis=0)
    squares = dot((stacked * stacked).astype(BF16), ones) * (1.0 / HEAD)
    unit = stacked * lax.rsqrt(squares + EPS) * head_gain
    value = dot(normed, block(2)).astype(BF16)
    exps, values = [], []
    for g in range(2):
        qg = (unit[g * FRAMES : (g + 1) * FRAMES] * (HEAD**-0.5)).astype(BF16)
        kg = unit[(2 + g) * FRAMES : (3 + g) * FRAMES].astype(BF16)
        vg = value[:, g * QUAD : (g + 1) * QUAD]
        keys = jnp.concatenate([kg * m for m in masks], axis=0)
        values.append(jnp.concatenate([vg * m for m in masks], axis=0))
        scores = lax.dot_general(qg, keys, (((1,), (1,)), ((), ())), preferred_element_type=F32)
        exps.append(jnp.where(causal, jnp.exp(scores), 0.0).astype(BF16))
    sums = dot(jnp.concatenate(exps, axis=0), ones)
    context = jnp.concatenate(
        [dot(exps[g], values[g]) / sums[g * FRAMES : (g + 1) * FRAMES] for g in range(2)], axis=1
    ).astype(BF16)
    total = dot(context, block(3))
    for half in range(2):
        up = dot(normed, block(4 + half))
        inner = 0.7978845608028654 * (up + 0.044715 * (up * up * up))
        hidden = (0.5 * up * (1.0 + jnp.tanh(inner))).astype(BF16)
        total = total + dot(hidden, block(6 + half))
    return total


def first_body(place, inputs, gains, w, base, moved, state):
    start = inputs[place[5]]
    change = delta(start, w, gains, place, 0)
    base[...] = STEP * (change + delta(start, w, gains, place, 1))
    after = start + STEP * change
    moved[...] = after + STEP * delta(after, w, gains, place, 1)
    state[...] = start


def rest_body(place, inputs, moved, base, gains, w, offset, term, kept):
    @pl.when(place[2] == 0)
    def _():
        offset[...] = -base[...]
        term[...] = jnp.zeros_like(term)
        kept[...] = jnp.zeros_like(kept)

    @pl.when(place[2] == 1)
    def _():
        state = moved[...]
        for i in range(2):
            state = state + STEP * delta(state, w, gains, place, i)
        offset[...] = state - inputs[place[5]] - base[...]
        term[...] = state
        kept[...] = state


def chain_body(low, high, half, place, v, gains, w, out):
    @pl.when((place[0] >= low) & (place[0] <= high) & (place[2] == half))
    def _():
        state = v[...]
        for i in range(2):
            state = state + STEP * delta(state, w, gains, place, i)
        out[...] = state


def coarse_body(turn, place, near, far, offset, gains, w, kept_in, state_in, term, kept, state):
    @pl.when(place[0] == turn)
    def _():
        value = near[...] + far[...]
        state[...] = value
        held = jnp.where(place[2] == 0, 1.0, 0.0).astype(F32)
        change = delta(value, w, gains, place, 0) + delta(value, w, gains, place, 1)
        share = held * value + offset[...] + STEP * change
        term[...] = share
        kept[...] = share


def final_body(place, inputs, handed, gains, w, state_0, state_1):
    @pl.when(place[2] == 0)
    def _():
        start = jnp.where(place[0] == 0, inputs[place[5]], handed[...])
        after = start + STEP * delta(start, w, gains, place, 0)
        state_0[...] = after
        state_1[...] = after + STEP * delta(after, w, gains, place, 1)


def pick_body(last, place, state_0, state_1, fresh, fresh_last, passed, gains, w, mine, send):
    odd = place[1] % 2

    def put(even, uneven):
        mine[...] = jnp.where(odd == 0, even, uneven)
        send[...] = jnp.where(odd == 0, uneven, even)

    @pl.when(place[2] == 0)
    def _():
        put(state_0[...], state_1[...])

    @pl.when(place[2] == 1)
    def _():
        state = passed[...]
        state = state + STEP * delta(state, w, gains, place, 0)
        put(state, jnp.where(place[0] == last, fresh_last[...], fresh[...]))


def both_body(place, *refs):
    second = place[5]
    for mine, got, out in zip(refs[0:4:2], refs[1:4:2], refs[4:], strict=True):
        out[second] = mine[...]
        out[1 - second] = got[...]


PARAMS = pltpu.CompilerParams(vmem_limit_bytes=12 * 2**20)
STATE = jax.ShapeDtypeStruct((FRAMES, WIDTH), F32)
PAIR = jax.ShapeDtypeStruct((2, FRAMES, WIDTH), F32)


def run(body, outs, place, *arrays, aliases=None, fixed=()):
    def kernel(*refs):
        body(*fixed, *refs)

    return pl.pallas_call(
        kernel,
        out_shape=outs,
        in_specs=[SMEM_SPEC] + [VMEM_SPEC] * len(arrays),
        out_specs=[VMEM_SPEC] * len(outs),
        input_output_aliases=aliases or {},
        compiler_params=PARAMS,
        name=body.__name__[:-5],
    )(place, *arrays)


def blocks_of(attn_in, attn_out, mlp_in, mlp_out):
    return (
        [attn_in.at[0, :, pl.ds(i * WIDTH, WIDTH)] for i in range(3)]
        + [attn_out.at[0]]
        + [mlp_in.at[0, :, pl.ds(i * WIDTH, WIDTH)] for i in range(2)]
        + [mlp_out.at[0, pl.ds(i * WIDTH, WIDTH), :] for i in range(2)]
    )


def pack_body(place, attn_in, attn_out, mlp_in, mlp_out, *rest):
    outs, (buffer, sem) = rest[:-2], rest[-2:]
    rows = ROWS // (4 * CHUNKS)
    blocks = blocks_of(attn_in, attn_out, mlp_in, mlp_out)
    quarter = place[3] * 2 + place[4]

    def copy(j, p):
        at = (4 * j + p) * rows
        source = blocks[at // WIDTH].at[pl.ds(at % WIDTH, rows), :]
        return pltpu.make_async_copy(source, buffer.at[j], sem.at[j])

    for j in range(CHUNKS):
        for p in range(4):
            pl.when(quarter == p)(copy(j, p).start)
    for j in range(CHUNKS):
        copy(j, 0).wait()
        outs[j][...] = buffer[j].astype(F32)


def pack(place, weights):
    rows = ROWS // (4 * CHUNKS)
    return pl.pallas_call(
        pack_body,
        out_shape=[jax.ShapeDtypeStruct((rows, WIDTH), F32)] * CHUNKS,
        in_specs=[SMEM_SPEC] + [HBM_SPEC] * 4,
        out_specs=[VMEM_SPEC] * CHUNKS,
        scratch_shapes=[
            pltpu.VMEM((CHUNKS, rows, WIDTH), BF16),
            pltpu.SemaphoreType.DMA((CHUNKS,)),
        ],
        compiler_params=pltpu.CompilerParams(vmem_limit_bytes=12 * 2**20),
        name="pack",
    )(place, *weights)


def load_body(place, attn_in, attn_out, mlp_in, mlp_out, *rest):
    pieces, (w, buffer, own_sem, sem) = rest[:-4], rest[-4:]
    piece_rows = ROWS // (4 * CHUNKS)
    slot = place[1] % 2
    own = blocks_of(attn_in, attn_out, mlp_in, mlp_out)
    copies = [
        pltpu.make_async_copy(src, w.at[slot, pl.ds(i * WIDTH, WIDTH), :], own_sem.at[i])
        for i, src in enumerate(own)
    ]
    for copy in copies:
        copy.start()
    parity, core = place[3], place[4]
    half = piece_rows // 2
    todo = []
    for j in range(CHUNKS):
        direct, lower, upper, swapped = pieces[4 * j : 4 * j + 4]
        base = j * 4 * piece_rows
        here = base + (parity * 2 + core) * piece_rows
        beside = base + ((1 - parity) * 2 + core) * piece_rows
        other = base + (parity * 2 + 1 - core) * piece_rows
        cross = base + ((1 - parity) * 2 + 1 - core) * piece_rows
        todo += [
            (direct.at[pl.ds(0, half)], here),
            (direct.at[pl.ds(half, half)], here + half),
            (lower, beside),
            (upper, beside + half),
            (swapped.at[pl.ds(0, half)], other),
            (swapped.at[pl.ds(half, half)], other + half),
            (swapped.at[pl.ds(2 * half, half)], cross),
            (swapped.at[pl.ds(3 * half, half)], cross + half),
        ]

    def fetch(i):
        return pltpu.make_async_copy(todo[i][0], buffer.at[i % 3], sem.at[i % 3])

    fetch(0).start()
    fetch(1).start()
    for i in range(len(todo)):
        if i + 2 < len(todo):
            fetch(i + 2).start()
        fetch(i).wait()
        at = pl.multiple_of(todo[i][1], half)
        w[1 - slot, pl.ds(at, half), :] = buffer[i % 3].astype(BF16)
    for copy in copies:
        copy.wait()


def load(place, weights, pieces):
    half = ROWS // (8 * CHUNKS)
    return pl.pallas_call(
        load_body,
        out_shape=pltpu.VMEM((2, ROWS, WIDTH), BF16),
        in_specs=[SMEM_SPEC] + [HBM_SPEC] * (4 + len(pieces)),
        out_specs=VMEM_SPEC,
        scratch_shapes=[
            pltpu.VMEM((3, half, WIDTH), F32),
            pltpu.SemaphoreType.DMA((8,)),
            pltpu.SemaphoreType.DMA((3,)),
        ],
        compiler_params=pltpu.CompilerParams(vmem_limit_bytes=8 * 2**20),
        name="load",
    )(place, *weights, *pieces)


def on_device(inputs, attn_in, attn_out, mlp_in, mlp_out, norm_gain, head_gain):
    layers, groups = lax.axis_size("depth"), lax.axis_size("batch")
    blocks = layers // COARSEN
    device, group = lax.axis_index("depth"), lax.axis_index("batch")
    z, x = device // COARSEN, device % COARSEN
    odd, half = x % 2, x // 2
    row, core = group // 2, group % 2
    parity = row % 2
    place = jnp.stack([z, x, half, parity, core, odd ^ half]).astype(jnp.int32)

    def move(array, pairs):
        return lax.ppermute(array, "depth", pairs)

    def within(array, source, by, low=0, high=blocks - 1):
        pairs = [
            (COARSEN * k + i, COARSEN * k + (i ^ by)) for k in range(low, high + 1) for i in source
        ]
        return move(array, pairs)

    own_gains = jnp.concatenate(
        [norm_gain, jnp.tile(head_gain, (1, WIDTH // HEAD)), jnp.zeros((6, WIDTH), F32)], axis=0
    )
    weights = tuple(
        pltpu.with_memory_space_constraint(a, pltpu.HBM)
        for a in (attn_in, attn_out, mlp_in, mlp_out)
    )
    packed = pack(place, weights)
    partner_gains = within(own_gains, range(COARSEN), 1)
    half_rows = ROWS // (8 * CHUNKS)
    rows = groups // 2
    onward = [(2 * r + c, 2 * ((r + 1) % rows) + c) for r in range(rows) for c in range(2)]
    back = [(2 * r + c, 2 * ((r - 1) % rows) + c) for r in range(rows) for c in range(2)]
    swap = [(g, g ^ 1) for g in range(groups)]
    pieces = []
    for j in range(CHUNKS):
        direct = within(packed[j], range(COARSEN), 1)
        lower = lax.ppermute(direct[:half_rows], "batch", onward)
        upper = lax.ppermute(direct[half_rows:], "batch", back)
        swapped = lax.ppermute(jnp.concatenate([direct, lower, upper], axis=0), "batch", swap)
        pieces += [direct, lower, upper, swapped]
    w = load(place, weights, [pltpu.with_memory_space_constraint(p, pltpu.HBM) for p in pieces])
    gains = jnp.concatenate([own_gains, partner_gains], axis=0)

    last = blocks - 1
    front, rear = (0, 1), (2, 3)
    base, moved, state = run(first_body, [STATE] * 3, place, inputs, gains, w)
    moved = within(moved, front, 3)
    offset, term, kept = run(rest_body, [STATE] * 3, place, inputs, moved, base, gains, w)
    for turn in range(1, blocks):
        pairs = [COARSEN * k + i for k in range((turn - 1) % 8, last, 8) for i in range(COARSEN)]
        near = move(term, [(p, p + COARSEN) for p in pairs])
        far = move(term, [(p, (p ^ 3) + COARSEN) for p in pairs])
        aliases = {6: 1, 7: 2} if turn < last else {6: 1}
        early = state
        term, kept, state = run(
            coarse_body, [STATE] * 3, place, near, far, offset, gains, w, kept, state,
            aliases=aliases, fixed=(turn,),
        )

    def relax(low, high, value):
        (middle,) = run(chain_body, [STATE], place, value, gains, w, fixed=(low, high, 0))
        middle = within(middle, front, 3, low, high)
        return run(chain_body, [STATE], place, middle, gains, w, fixed=(low, high, 1))[0]

    fresh = relax(0, last - 1, early)
    handed = move(
        fresh, [(COARSEN * k + i, COARSEN * (k + 1) + (i ^ 3)) for k in range(last) for i in rear]
    )
    fresh_last = relax(last, last, state)
    state_0, state_1 = run(final_body, [STATE] * 2, place, inputs, handed, gains, w)
    mine, send = run(
        pick_body, [STATE] * 2, place, state_0, state_1, fresh, fresh_last,
        within(state_1, front, 3), gains, w, fixed=(last,),
    )

    everyone = range(COARSEN)
    corrected = kept + within(kept, everyone, 3)
    output, ahead = run(
        both_body, [PAIR] * 2, place, mine, within(send, everyone, 1), corrected,
        within(corrected, everyone, 1),
    )
    return (output[None], ahead[None])


def solution(mesh):
    in_specs = (
        P("batch", None, None),
        P("depth", None, None),
        P("depth", None, None),
        P("depth", None, None),
        P("depth", None, None),
        P("depth", None),
        P("depth", None),
    )
    out_specs = (P("depth", "batch", None, None), P("depth", "batch", None, None))
    return jax.shard_map(
        on_device, mesh=mesh, in_specs=in_specs, out_specs=out_specs, check_vma=False
    )
```

```python
import jax
import jax.numpy as jnp
from jax import lax
from jax.experimental import pallas as pl
from jax.experimental.pallas import tpu as pltpu
from jax.sharding import PartitionSpec as P

F32, BF16 = jnp.float32, jnp.bfloat16
COARSEN = 4
STEP = 0.25
EPS = 1e-6
FRAMES, WIDTH, HEAD = 64, 512, 64
ROWS = 4096
CHUNKS = (1408, 1408, 1280)
QUAD = 4 * HEAD
VMEM_SPEC = pl.BlockSpec(memory_space=pltpu.VMEM)
HBM_SPEC = pl.BlockSpec(memory_space=pltpu.HBM)


def dot(left, right):
    return jnp.dot(left, right, preferred_element_type=F32)


def where_am_i():
    device = lax.axis_index("depth")
    x = device % COARSEN
    return device // COARSEN, x, x % 2, x // 2, x % 2 ^ x // 2


def gelu(up):
    return (0.5 * up * (1.0 + jnp.tanh(0.7978845608028654 * (up + 0.044715 * (up * up * up))))).astype(BF16)


def deltas(v, w, gains, odd, layers):
    row = lax.broadcasted_iota(jnp.int32, (FRAMES, QUAD), 0)
    lane = lax.broadcasted_iota(jnp.int32, (FRAMES, QUAD), 1)
    causal = row >= lane % HEAD
    masks = [jnp.where(lane // HEAD == h, 1.0, 0.0).astype(BF16) for h in range(4)]
    ones = jnp.where(
        lax.broadcasted_iota(jnp.int32, (QUAD, QUAD), 0) // HEAD
        == lax.broadcasted_iota(jnp.int32, (QUAD, QUAD), 1) // HEAD,
        1.0,
        0.0,
    ).astype(BF16)
    each = range(len(layers))

    def block(n, i):
        return w[layers[n], i * WIDTH : (i + 1) * WIDTH, :]

    def rows(array, i):
        return array[i * FRAMES : (i + 1) * FRAMES]

    at = [(odd + layer) % 2 * 8 for layer in layers]
    scaled = v * lax.rsqrt(jnp.mean(v * v, axis=-1, keepdims=True) + EPS)
    normed = [(scaled * gains[pl.ds(at[n], 1), :]).astype(BF16) for n in each]
    stacked = []
    for n in each:
        both = [dot(normed[n], block(n, i)) for i in range(2)]
        stacked.append(jnp.concatenate([p[:, g : g + QUAD] for p in both for g in (0, QUAD)], axis=0))
    squares = [dot((s * s).astype(BF16), ones) * (1.0 / HEAD) for s in stacked]
    value = [dot(normed[n], block(n, 2)).astype(BF16) for n in each]
    up = [[dot(normed[n], block(n, 4 + i)) for i in range(2)] for n in each]
    exps, values = [], []
    for n in each:
        head_gain = gains[pl.ds(at[n] + 1, 1), :QUAD]
        unit = stacked[n] * lax.rsqrt(squares[n] + EPS) * head_gain
        for g in range(2):
            query = (rows(unit, g) * (HEAD**-0.5)).astype(BF16)
            key = rows(unit, 2 + g).astype(BF16)
            keys = jnp.concatenate([key * m for m in masks], axis=0)
            part = value[n][:, g * QUAD : (g + 1) * QUAD]
            values.append(jnp.concatenate([part * m for m in masks], axis=0))
            scores = lax.dot_general(
                query, keys, (((1,), (1,)), ((), ())), preferred_element_type=F32
            )
            exps.append(jnp.where(causal, jnp.exp(scores), 0.0).astype(BF16))
    total = None
    hidden = [[gelu(u) for u in up[n]] for n in each]
    for n in each:
        down = dot(hidden[n][0], block(n, 6)) + dot(hidden[n][1], block(n, 7))
        total = down if total is None else total + down
    sums = dot(jnp.concatenate(exps, axis=0), ones)
    for n in each:
        context = jnp.concatenate(
            [dot(exps[i], values[i]) / rows(sums, i) for i in (2 * n, 2 * n + 1)], axis=1
        ).astype(BF16)
        total = total + dot(context, block(n, 3))
    return total


def advance(v, w, gains, odd, layer):
    return v + STEP * deltas(v, w, gains, odd, (layer,))


def first_body(inputs, gains, w, moved, state):
    z, x, odd, half, second = where_am_i()
    start = inputs[second]
    moved[...] = advance(advance(start, w, gains, odd, 0), w, gains, odd, 1)
    state[...] = start


def base_body(state, gains, w, base):
    z, x, odd, half, second = where_am_i()
    base[...] = STEP * deltas(state[...], w, gains, odd, (0, 1))


def rest_body(start, moved, base, gains, w, offset, term, kept):
    z, x, odd, half, second = where_am_i()

    @pl.when(half == 0)
    def _():
        offset[...] = -base[...]
        term[...] = jnp.zeros_like(term)
        kept[...] = jnp.zeros_like(kept)

    @pl.when(half == 1)
    def _():
        state = advance(advance(moved[...], w, gains, odd, 0), w, gains, odd, 1)
        offset[...] = state - start[...] - base[...]
        term[...] = state
        kept[...] = state


def chain_body(low, high, side, v, gains, w, out):
    z, x, odd, half, second = where_am_i()

    @pl.when((z >= low) & (z <= high) & (half == side))
    def _():
        out[...] = advance(advance(v[...], w, gains, odd, 0), w, gains, odd, 1)


def coarse_body(turn, near, far, offset, gains, w, kept_in, state_in, term, kept, state):
    z, x, odd, half, second = where_am_i()

    @pl.when(z == turn)
    def _():
        value = near[...] + far[...]
        state[...] = value
        held = jnp.where(half == 0, 1.0, 0.0).astype(F32)
        share = held * value + offset[...] + STEP * deltas(value, w, gains, odd, (0, 1))
        term[...] = share
        kept[...] = share


def final_body(start, handed, gains, w, state_0, state_1):
    z, x, odd, half, second = where_am_i()

    @pl.when(half == 0)
    def _():
        begin = jnp.where(z == 0, start[...], handed[...])
        after = advance(begin, w, gains, odd, 0)
        state_0[...] = after
        state_1[...] = advance(after, w, gains, odd, 1)


def pick_body(last, state_0, state_1, fresh, fresh_last, passed, gains, w, mine, send):
    z, x, odd, half, second = where_am_i()

    def put(even, uneven):
        mine[...] = jnp.where(odd == 0, even, uneven)
        send[...] = jnp.where(odd == 0, uneven, even)

    @pl.when(half == 0)
    def _():
        put(state_0[...], state_1[...])

    @pl.when(half == 1)
    def _():
        state = advance(passed[...], w, gains, odd, 0)
        put(state, jnp.where(z == last, fresh_last[...], fresh[...]))


def both_body(*refs):
    z, x, odd, half, second = where_am_i()
    for mine, got, out in zip(refs[0:4:2], refs[1:4:2], refs[4:], strict=True):
        out[second] = mine[...]
        out[1 - second] = got[...]


PARAMS = pltpu.CompilerParams(vmem_limit_bytes=12 * 2**20)
STATE = jax.ShapeDtypeStruct((FRAMES, WIDTH), F32)
PAIR = jax.ShapeDtypeStruct((2, FRAMES, WIDTH), F32)


def run(body, outs, *arrays, aliases=None, fixed=()):
    def kernel(*refs):
        body(*fixed, *refs)

    return pl.pallas_call(
        kernel,
        out_shape=outs,
        in_specs=[VMEM_SPEC] * len(arrays),
        out_specs=[VMEM_SPEC] * len(outs),
        input_output_aliases=aliases or {},
        compiler_params=PARAMS,
        name=body.__name__[:-5],
    )(*arrays)


def quarter():
    group = lax.axis_index("batch")
    return group // 2 % 2, group % 2


def own_piece(w, slot, base, chunk):
    parity, core = quarter()
    at = pl.multiple_of(base + (parity * 2 + core) * (chunk // 4), 32)
    return w[slot, pl.ds(at, chunk // 4), :].astype(F32)


def piece_shape(chunk):
    return jax.ShapeDtypeStruct((chunk // 4, WIDTH), F32)


def pack_body(attn_in, attn_out, mlp_in, mlp_out, norm_gain, head_gain, w, gains, *rest):
    outs, sem = rest[:-1], rest[-1]
    slot = where_am_i()[2]
    blocks = (
        [attn_in.at[0, :, pl.ds(i * WIDTH, WIDTH)] for i in range(3)]
        + [attn_out.at[0]]
        + [mlp_in.at[0, :, pl.ds(i * WIDTH, WIDTH)] for i in range(2)]
        + [mlp_out.at[0, pl.ds(i * WIDTH, WIDTH), :] for i in range(2)]
    )
    copies = [
        pltpu.make_async_copy(source, w.at[slot, pl.ds(i * WIDTH, WIDTH), :], sem.at[i])
        for i, source in enumerate(blocks)
    ]
    for copy in copies:
        copy.start()
    for copy in copies:
        copy.wait()
    head = jnp.concatenate([head_gain[...]] * (WIDTH // HEAD), axis=1)
    gains[...] = jnp.concatenate([norm_gain[...], head, jnp.zeros((6, WIDTH), F32)], axis=0)
    base = 0
    for chunk, out in zip(CHUNKS, outs, strict=True):
        out[...] = own_piece(w, slot, base, chunk)
        base += chunk


def pack(weights):
    return pl.pallas_call(
        pack_body,
        out_shape=[pltpu.VMEM((2, ROWS, WIDTH), BF16), jax.ShapeDtypeStruct((8, WIDTH), F32)]
        + [piece_shape(chunk) for chunk in CHUNKS],
        in_specs=[HBM_SPEC] * 4 + [VMEM_SPEC] * 2,
        out_specs=[VMEM_SPEC] * (2 + len(CHUNKS)),
        scratch_shapes=[pltpu.SemaphoreType.DMA((8,))],
        compiler_params=PARAMS,
        name="pack",
    )(*weights)


def load_body(base, chunk, w_in, direct, beside, direct_swapped, beside_swapped, w):
    slot = 1 - where_am_i()[2]
    parity, core = quarter()
    for piece, number in (
        (direct, parity * 2 + core),
        (beside, (1 - parity) * 2 + core),
        (direct_swapped, parity * 2 + 1 - core),
        (beside_swapped, (1 - parity) * 2 + 1 - core),
    ):
        at = pl.multiple_of(base + number * (chunk // 4), 32)
        w[slot, pl.ds(at, chunk // 4), :] = piece[...].astype(BF16)


def load(base, chunk, w, *pieces):
    return run(
        load_body, [pltpu.VMEM((2, ROWS, WIDTH), BF16)], w, *pieces,
        aliases={0: 0}, fixed=(base, chunk),
    )[0]


def join_body(own, partner, out):
    out[...] = jnp.concatenate([own[...], partner[...]], axis=0)


def on_device(inputs, attn_in, attn_out, mlp_in, mlp_out, norm_gain, head_gain):
    layers, groups = lax.axis_size("depth"), lax.axis_size("batch")
    blocks = layers // COARSEN
    last = blocks - 1
    everyone, front, rear = range(COARSEN), (0, 1), (2, 3)
    def move(array, pairs):
        return lax.ppermute(array, "depth", pairs)

    def within(array, source, by, low=0, high=blocks - 1):
        pairs = [
            (COARSEN * k + i, COARSEN * k + (i ^ by)) for k in range(low, high + 1) for i in source
        ]
        return move(array, pairs)

    weights = tuple(
        pltpu.with_memory_space_constraint(a, pltpu.HBM)
        for a in (attn_in, attn_out, mlp_in, mlp_out)
    )
    w, own_gains, *packed = pack(weights + (norm_gain, head_gain))
    partner_gains = within(own_gains, everyone, 1)
    (gains,) = run(join_body, [jax.ShapeDtypeStruct((16, WIDTH), F32)], own_gains, partner_gains)
    rows = groups // 2
    pairings = [
        [(2 * (r ^ 1) + c, 2 * r + c) for r in range(rows) for c in range(2)],
        [(2 * ((((r + 1) % rows) ^ 1) - 1) % groups + c, 2 * r + c) for r in range(rows) for c in range(2)],
    ]
    swap = [(g, g ^ 1) for g in range(groups)]
    base = 0
    for j, chunk in enumerate(CHUNKS):
        direct = within(packed[j], everyone, 1)
        beside = lax.ppermute(direct, "batch", pairings[j % 2])
        direct_swapped = lax.ppermute(direct, "batch", swap)
        beside_swapped = lax.ppermute(beside, "batch", swap)
        w = load(base, chunk, w, direct, beside, direct_swapped, beside_swapped)
        base += chunk

    moved, start = run(first_body, [STATE] * 2, inputs, gains, w)
    moved = within(moved, front, 3)
    (base,) = run(base_body, [STATE], start, gains, w)
    offset, term, kept = run(rest_body, [STATE] * 3, start, moved, base, gains, w)
    state = start
    for turn in range(1, blocks):
        pairs = [COARSEN * k + i for k in range((turn - 1) % 8, last, 8) for i in range(COARSEN)]
        near = move(term, [(p, p + COARSEN) for p in pairs])
        far = move(term, [(p, (p ^ 3) + COARSEN) for p in pairs])
        aliases = {5: 1, 6: 2} if turn < last else {5: 1}
        early = state
        term, kept, state = run(
            coarse_body, [STATE] * 3, near, far, offset, gains, w, kept, state,
            aliases=aliases, fixed=(turn,),
        )

    def relax(low, high, value):
        (middle,) = run(chain_body, [STATE], value, gains, w, fixed=(low, high, 0))
        middle = within(middle, front, 3, low, high)
        return run(chain_body, [STATE], middle, gains, w, fixed=(low, high, 1))[0]

    fresh = relax(0, last - 1, early)
    handed = move(
        fresh, [(COARSEN * k + i, COARSEN * (k + 1) + (i ^ 3)) for k in range(last) for i in rear]
    )
    fresh_last = relax(last, last, state)
    state_0, state_1 = run(final_body, [STATE] * 2, start, handed, gains, w)
    mine, send = run(
        pick_body, [STATE] * 2, state_0, state_1, fresh, fresh_last,
        within(state_1, front, 3), gains, w, fixed=(last,),
    )

    corrected = kept + within(kept, everyone, 3)
    output, ahead = run(
        both_body, [PAIR] * 2, mine, within(send, everyone, 1), corrected,
        within(corrected, everyone, 1),
    )
    return (output[None], ahead[None])


def solution(mesh):
    in_specs = (
        P("batch", None, None),
        P("depth", None, None),
        P("depth", None, None),
        P("depth", None, None),
        P("depth", None, None),
        P("depth", None),
        P("depth", None),
    )
    out_specs = (P("depth", "batch", None, None), P("depth", "batch", None, None))
    return jax.shard_map(
        on_device, mesh=mesh, in_specs=in_specs, out_specs=out_specs, check_vma=False
    )
```

```python
import jax
import jax.numpy as jnp
from jax import lax
from jax.experimental import pallas as pl
from jax.experimental.pallas import tpu as pltpu
from jax.sharding import PartitionSpec as P

F32, BF16 = jnp.float32, jnp.bfloat16
COARSEN = 4
STEP = 0.25
EPS = 1e-6
FRAMES, WIDTH, HEAD = 64, 512, 64
ROWS = 4096
CHUNKS = (1664, 1408, 1024)
PIECES = [chunk // 4 + (8 if j == 0 else 0) for j, chunk in enumerate(CHUNKS)]
QUAD = 4 * HEAD
VMEM_SPEC = pl.BlockSpec(memory_space=pltpu.VMEM)
HBM_SPEC = pl.BlockSpec(memory_space=pltpu.HBM)


def dot(left, right):
    return jnp.dot(left, right, preferred_element_type=F32)


def where_am_i():
    device = lax.axis_index("depth")
    x = device % COARSEN
    return device // COARSEN, x, x % 2, x // 2, x % 2 ^ x // 2


def gelu(up):
    return (0.5 * up * (1.0 + jnp.tanh(0.7978845608028654 * (up + 0.044715 * (up * up * up))))).astype(BF16)


def deltas(v, w, gains, odd, layers):
    row = lax.broadcasted_iota(jnp.int32, (FRAMES, QUAD), 0)
    lane = lax.broadcasted_iota(jnp.int32, (FRAMES, QUAD), 1)
    causal = row >= lane % HEAD
    masks = [jnp.where(lane // HEAD == h, 1.0, 0.0).astype(BF16) for h in range(4)]
    ones = jnp.where(
        lax.broadcasted_iota(jnp.int32, (QUAD, QUAD), 0) // HEAD
        == lax.broadcasted_iota(jnp.int32, (QUAD, QUAD), 1) // HEAD,
        1.0,
        0.0,
    ).astype(BF16)
    each = range(len(layers))

    def block(n, i):
        return w[layers[n], i * WIDTH : (i + 1) * WIDTH, :]

    def rows(array, i):
        return array[i * FRAMES : (i + 1) * FRAMES]

    at = [(odd + layer) % 2 * 8 for layer in layers]
    scaled = v * lax.rsqrt(jnp.mean(v * v, axis=-1, keepdims=True) + EPS)
    normed = [(scaled * gains[pl.ds(at[n], 1), :]).astype(BF16) for n in each]
    stacked = []
    for n in each:
        both = [dot(normed[n], block(n, i)) for i in range(2)]
        stacked.append(jnp.concatenate([p[:, g : g + QUAD] for p in both for g in (0, QUAD)], axis=0))
    squares = [dot((s * s).astype(BF16), ones) * (1.0 / HEAD) for s in stacked]
    value = [dot(normed[n], block(n, 2)).astype(BF16) for n in each]
    up = [[dot(normed[n], block(n, 4 + i)) for i in range(2)] for n in each]
    exps, values = [], []
    for n in each:
        head_gain = gains[pl.ds(at[n] + 1, 1), :QUAD]
        unit = stacked[n] * lax.rsqrt(squares[n] + EPS) * head_gain
        for g in range(2):
            query = (rows(unit, g) * (HEAD**-0.5)).astype(BF16)
            key = rows(unit, 2 + g).astype(BF16)
            keys = jnp.concatenate([key * m for m in masks], axis=0)
            part = value[n][:, g * QUAD : (g + 1) * QUAD]
            values.append(jnp.concatenate([part * m for m in masks], axis=0))
            scores = lax.dot_general(
                query, keys, (((1,), (1,)), ((), ())), preferred_element_type=F32
            )
            exps.append(jnp.where(causal, jnp.exp(scores), 0.0).astype(BF16))
    total = None
    hidden = [[gelu(u) for u in up[n]] for n in each]
    for n in each:
        down = dot(hidden[n][0], block(n, 6)) + dot(hidden[n][1], block(n, 7))
        total = down if total is None else total + down
    sums = dot(jnp.concatenate(exps, axis=0), ones)
    for n in each:
        context = jnp.concatenate(
            [dot(exps[i], values[i]) / rows(sums, i) for i in (2 * n, 2 * n + 1)], axis=1
        ).astype(BF16)
        total = total + dot(context, block(n, 3))
    return total


def advance(v, w, gains, odd, layer):
    return v + STEP * deltas(v, w, gains, odd, (layer,))


def first_body(inputs, gains, w, moved, state):
    z, x, odd, half, second = where_am_i()
    start = inputs[second]
    moved[...] = advance(advance(start, w, gains, odd, 0), w, gains, odd, 1)
    state[...] = start


def base_body(state, gains, w, base):
    z, x, odd, half, second = where_am_i()
    base[...] = STEP * deltas(state[...], w, gains, odd, (0, 1))


def rest_body(start, moved, base, gains, w, offset, term, kept):
    z, x, odd, half, second = where_am_i()

    @pl.when(half == 0)
    def _():
        offset[...] = -base[...]
        term[...] = jnp.zeros_like(term)
        kept[...] = jnp.zeros_like(kept)

    @pl.when(half == 1)
    def _():
        state = advance(advance(moved[...], w, gains, odd, 0), w, gains, odd, 1)
        offset[...] = state - start[...] - base[...]
        term[...] = state
        kept[...] = state


def chain_body(low, high, side, v, gains, w, out):
    z, x, odd, half, second = where_am_i()

    @pl.when((z >= low) & (z <= high) & (half == side))
    def _():
        out[...] = advance(advance(v[...], w, gains, odd, 0), w, gains, odd, 1)


def coarse_body(turn, far, near, offset, gains, w, kept_in, state_in, term, kept, state):
    z, x, odd, half, second = where_am_i()

    @pl.when(z == turn)
    def _():
        value = near[...] + far[...]
        state[...] = value
        held = jnp.where(half == 0, 1.0, 0.0).astype(F32)
        share = held * value + offset[...] + STEP * deltas(value, w, gains, odd, (0, 1))
        term[...] = share
        kept[...] = share


def final_body(start, handed, gains, w, kept_in, state_0, state_1, kept):
    z, x, odd, half, second = where_am_i()
    kept[...] = kept_in[...]

    @pl.when(half == 0)
    def _():
        begin = jnp.where(z == 0, start[...], handed[...])
        after = advance(begin, w, gains, odd, 0)
        state_0[...] = after
        state_1[...] = advance(after, w, gains, odd, 1)


def pick_body(last, state_0, state_1, fresh, fresh_last, passed, gains, w, mine, send):
    z, x, odd, half, second = where_am_i()

    def put(even, uneven):
        mine[...] = jnp.where(odd == 0, even, uneven)
        send[...] = jnp.where(odd == 0, uneven, even)

    @pl.when(half == 0)
    def _():
        put(state_0[...], state_1[...])

    @pl.when(half == 1)
    def _():
        state = advance(passed[...], w, gains, odd, 0)
        put(state, jnp.where(z == last, fresh_last[...], fresh[...]))


def both_body(*refs):
    z, x, odd, half, second = where_am_i()
    for mine, got, out in zip(refs[0:4:2], refs[1:4:2], refs[4:], strict=True):
        out[second] = mine[...]
        out[1 - second] = got[...]


PARAMS = pltpu.CompilerParams(vmem_limit_bytes=12 * 2**20)
STATE = jax.ShapeDtypeStruct((FRAMES, WIDTH), F32)
PAIR = jax.ShapeDtypeStruct((2, FRAMES, WIDTH), F32)


def run(body, outs, *arrays, aliases=None, fixed=()):
    def kernel(*refs):
        body(*fixed, *refs)

    return pl.pallas_call(
        kernel,
        out_shape=outs,
        in_specs=[VMEM_SPEC] * len(arrays),
        out_specs=[VMEM_SPEC] * len(outs),
        input_output_aliases=aliases or {},
        compiler_params=PARAMS,
        name=body.__name__[:-5],
    )(*arrays)


def quarter():
    group = lax.axis_index("batch")
    return group // 2 % 2, group % 2


def own_piece(w, slot, base, chunk):
    parity, core = quarter()
    at = pl.multiple_of(base + (parity * 2 + core) * (chunk // 4), 32)
    return w[slot, pl.ds(at, chunk // 4), :].astype(F32)


def pack_body(attn_in, attn_out, mlp_in, mlp_out, norm_gain, head_gain, w, gains, *rest):
    outs, sem = rest[:-1], rest[-1]
    slot = where_am_i()[2]
    blocks = (
        [attn_in.at[0, :, pl.ds(i * WIDTH, WIDTH)] for i in range(3)]
        + [attn_out.at[0]]
        + [mlp_in.at[0, :, pl.ds(i * WIDTH, WIDTH)] for i in range(2)]
        + [mlp_out.at[0, pl.ds(i * WIDTH, WIDTH), :] for i in range(2)]
    )
    copies = [
        pltpu.make_async_copy(source, w.at[slot, pl.ds(i * WIDTH, WIDTH), :], sem.at[i])
        for i, source in enumerate(blocks)
    ]
    for copy in copies:
        copy.start()
    for copy in copies:
        copy.wait()
    head = jnp.concatenate([head_gain[...]] * (WIDTH // HEAD), axis=1)
    gains[...] = jnp.concatenate([norm_gain[...], head, jnp.zeros((6, WIDTH), F32)], axis=0)
    base = 0
    for chunk, out in zip(CHUNKS, outs, strict=True):
        out[: chunk // 4] = own_piece(w, slot, base, chunk)
        base += chunk
    outs[0][CHUNKS[0] // 4 :] = gains[...]


def pack(weights):
    return pl.pallas_call(
        pack_body,
        out_shape=[pltpu.VMEM((2, ROWS, WIDTH), BF16), jax.ShapeDtypeStruct((8, WIDTH), F32)]
        + [jax.ShapeDtypeStruct((rows, WIDTH), F32) for rows in PIECES],
        in_specs=[HBM_SPEC] * 4 + [VMEM_SPEC] * 2,
        out_specs=[VMEM_SPEC] * (2 + len(CHUNKS)),
        scratch_shapes=[pltpu.SemaphoreType.DMA((8,))],
        compiler_params=PARAMS,
        name="pack",
    )(*weights)


def load_body(base, chunk, w_in, direct, beside, direct_swapped, beside_swapped, w):
    slot = 1 - where_am_i()[2]
    parity, core = quarter()
    for piece, number in (
        (direct, parity * 2 + core),
        (beside, (1 - parity) * 2 + core),
        (direct_swapped, parity * 2 + 1 - core),
        (beside_swapped, (1 - parity) * 2 + 1 - core),
    ):
        at = pl.multiple_of(base + number * (chunk // 4), 32)
        w[slot, pl.ds(at, chunk // 4), :] = piece[: chunk // 4].astype(BF16)


def load(base, chunk, w, *pieces):
    return run(
        load_body, [pltpu.VMEM((2, ROWS, WIDTH), BF16)], w, *pieces,
        aliases={0: 0}, fixed=(base, chunk),
    )[0]


def join_body(own, partner, out):
    out[...] = jnp.concatenate([own[...], partner[CHUNKS[0] // 4 :]], axis=0)


def on_device(inputs, attn_in, attn_out, mlp_in, mlp_out, norm_gain, head_gain):
    layers, groups = lax.axis_size("depth"), lax.axis_size("batch")
    blocks = layers // COARSEN
    last = blocks - 1
    everyone, front, rear = range(COARSEN), (0, 1), (2, 3)
    def move(array, pairs):
        return lax.ppermute(array, "depth", pairs)

    def within(array, source, by, low=0, high=blocks - 1):
        pairs = [
            (COARSEN * k + i, COARSEN * k + (i ^ by)) for k in range(low, high + 1) for i in source
        ]
        return move(array, pairs)

    weights = tuple(
        pltpu.with_memory_space_constraint(a, pltpu.HBM)
        for a in (attn_in, attn_out, mlp_in, mlp_out)
    )
    w, own_gains, *packed = pack(weights + (norm_gain, head_gain))
    rows = groups // 2
    pairings = [
        [(2 * (r ^ 1) + c, 2 * r + c) for r in range(rows) for c in range(2)],
        [(2 * ((((r + 1) % rows) ^ 1) - 1) % groups + c, 2 * r + c) for r in range(rows) for c in range(2)],
    ]
    swap = [(g, g ^ 1) for g in range(groups)]
    base = 0
    for j, chunk in enumerate(CHUNKS):
        direct = within(packed[j], everyone, 1)
        if j == 0:
            (gains,) = run(join_body, [jax.ShapeDtypeStruct((16, WIDTH), F32)], own_gains, direct)
        beside = lax.ppermute(direct, "batch", pairings[j % 2])
        direct_swapped = lax.ppermute(direct, "batch", swap)
        beside_swapped = lax.ppermute(beside, "batch", swap)
        w = load(base, chunk, w, direct, beside, direct_swapped, beside_swapped)
        base += chunk

    moved, start = run(first_body, [STATE] * 2, inputs, gains, w)
    moved = within(moved, front, 3)
    (base,) = run(base_body, [STATE], start, gains, w)
    offset, term, kept = run(rest_body, [STATE] * 3, start, moved, base, gains, w)
    state = start
    for turn in range(1, blocks):
        pairs = [COARSEN * k + i for k in range((turn - 1) % 8, last, 8) for i in range(COARSEN)]
        far = move(term, [(p, (p ^ 3) + COARSEN) for p in pairs])
        near = move(term, [(p, p + COARSEN) for p in pairs])
        aliases = {5: 1, 6: 2} if turn < last else {5: 1}
        early = state
        term, kept, state = run(
            coarse_body, [STATE] * 3, far, near, offset, gains, w, kept, state,
            aliases=aliases, fixed=(turn,),
        )

    def relax(low, high, value):
        (middle,) = run(chain_body, [STATE], value, gains, w, fixed=(low, high, 0))
        middle = within(middle, front, 3, low, high)
        return run(chain_body, [STATE], middle, gains, w, fixed=(low, high, 1))[0]

    fresh = relax(0, last - 1, early)
    handed = move(
        fresh, [(COARSEN * k + i, COARSEN * (k + 1) + (i ^ 3)) for k in range(last) for i in rear]
    )
    fresh_last = relax(last, last, state)
    state_0, state_1, kept = run(final_body, [STATE] * 3, start, handed, gains, w, kept)
    mine, send = run(
        pick_body, [STATE] * 2, state_0, state_1, fresh, fresh_last,
        within(state_1, front, 3), gains, w, fixed=(last,),
    )

    corrected = kept + within(kept, everyone, 3)
    output, ahead = run(
        both_body, [PAIR] * 2, mine, within(send, everyone, 1), corrected,
        within(corrected, everyone, 1),
    )
    return (output[None], ahead[None])


def solution(mesh):
    in_specs = (
        P("batch", None, None),
        P("depth", None, None),
        P("depth", None, None),
        P("depth", None, None),
        P("depth", None, None),
        P("depth", None),
        P("depth", None),
    )
    out_specs = (P("depth", "batch", None, None), P("depth", "batch", None, None))
    return jax.shard_map(
        on_device, mesh=mesh, in_specs=in_specs, out_specs=out_specs, check_vma=False
    )
```

```python
import jax
import jax.numpy as jnp
from jax import lax
from jax.experimental import pallas as pl
from jax.experimental.pallas import tpu as pltpu
from jax.sharding import PartitionSpec as P

F32, BF16 = jnp.float32, jnp.bfloat16
COARSEN = 4
STEP = 0.25
EPS = 1e-6
FRAMES, WIDTH, HEAD = 64, 512, 64
ROWS = 4096
CHUNKS = (1664, 1408, 1024)
PIECES = [chunk // 4 + (8 if j == 0 else 0) for j, chunk in enumerate(CHUNKS)]
QUAD = 4 * HEAD
VMEM_SPEC = pl.BlockSpec(memory_space=pltpu.VMEM)
HBM_SPEC = pl.BlockSpec(memory_space=pltpu.HBM)


def dot(left, right):
    return jnp.dot(left, right, preferred_element_type=F32)


def where_am_i():
    device = lax.axis_index("depth")
    x = device % COARSEN
    return device // COARSEN, x, x % 2, x // 2, x % 2 ^ x // 2


def gelu(up):
    return (0.5 * up * (1.0 + jnp.tanh(0.7978845608028654 * (up + 0.044715 * (up * up * up))))).astype(BF16)


def deltas(v, w, gains, odd, layers):
    row = lax.broadcasted_iota(jnp.int32, (FRAMES, QUAD), 0)
    lane = lax.broadcasted_iota(jnp.int32, (FRAMES, QUAD), 1)
    causal = row >= lane % HEAD
    masks = [jnp.where(lane // HEAD == h, 1.0, 0.0).astype(BF16) for h in range(4)]
    ones = jnp.where(
        lax.broadcasted_iota(jnp.int32, (QUAD, QUAD), 0) // HEAD
        == lax.broadcasted_iota(jnp.int32, (QUAD, QUAD), 1) // HEAD,
        1.0,
        0.0,
    ).astype(BF16)
    each = range(len(layers))

    def block(n, i):
        return w[layers[n], i * WIDTH : (i + 1) * WIDTH, :]

    def rows(array, i):
        return array[i * FRAMES : (i + 1) * FRAMES]

    at = [(odd + layer) % 2 * 8 for layer in layers]
    scaled = v * lax.rsqrt(jnp.mean(v * v, axis=-1, keepdims=True) + EPS)
    normed = [(scaled * gains[pl.ds(at[n], 1), :]).astype(BF16) for n in each]
    stacked = []
    for n in each:
        both = [dot(normed[n], block(n, i)) for i in range(2)]
        stacked.append(jnp.concatenate([p[:, g : g + QUAD] for p in both for g in (0, QUAD)], axis=0))
    squares = [dot((s * s).astype(BF16), ones) * (1.0 / HEAD) for s in stacked]
    value = [dot(normed[n], block(n, 2)).astype(BF16) for n in each]
    up = [[dot(normed[n], block(n, 4 + i)) for i in range(2)] for n in each]
    exps, values = [], []
    for n in each:
        head_gain = gains[pl.ds(at[n] + 1, 1), :QUAD]
        unit = stacked[n] * lax.rsqrt(squares[n] + EPS) * head_gain
        for g in range(2):
            query = (rows(unit, g) * (HEAD**-0.5)).astype(BF16)
            key = rows(unit, 2 + g).astype(BF16)
            keys = jnp.concatenate([key * m for m in masks], axis=0)
            part = value[n][:, g * QUAD : (g + 1) * QUAD]
            values.append(jnp.concatenate([part * m for m in masks], axis=0))
            scores = lax.dot_general(
                query, keys, (((1,), (1,)), ((), ())), preferred_element_type=F32
            )
            exps.append(jnp.where(causal, jnp.exp(scores), 0.0).astype(BF16))
    total = None
    hidden = [[gelu(u) for u in up[n]] for n in each]
    for n in each:
        down = dot(hidden[n][0], block(n, 6)) + dot(hidden[n][1], block(n, 7))
        total = down if total is None else total + down
    sums = dot(jnp.concatenate(exps, axis=0), ones)
    for n in each:
        context = jnp.concatenate(
            [dot(exps[i], values[i]) / rows(sums, i) for i in (2 * n, 2 * n + 1)], axis=1
        ).astype(BF16)
        total = total + dot(context, block(n, 3))
    return total


def advance(v, w, gains, odd, layer):
    return v + STEP * deltas(v, w, gains, odd, (layer,))


def first_body(inputs, gains, w, moved, state):
    z, x, odd, half, second = where_am_i()
    start = inputs[second]
    state[...] = start

    @pl.when(half == 0)
    def _():
        moved[...] = advance(advance(start, w, gains, odd, 0), w, gains, odd, 1)


def base_body(state, gains, w, base):
    z, x, odd, half, second = where_am_i()
    base[...] = STEP * deltas(state[...], w, gains, odd, (0, 1))


def rest_body(start, moved, base, gains, w, offset, term, kept):
    z, x, odd, half, second = where_am_i()

    @pl.when(half == 0)
    def _():
        offset[...] = -base[...]
        term[...] = jnp.zeros_like(term)
        kept[...] = jnp.zeros_like(kept)

    @pl.when(half == 1)
    def _():
        state = advance(advance(moved[...], w, gains, odd, 0), w, gains, odd, 1)
        offset[...] = state - start[...] - base[...]
        term[...] = state
        kept[...] = state


def chain_body(low, high, side, v, gains, w, out):
    z, x, odd, half, second = where_am_i()

    @pl.when((z >= low) & (z <= high) & (half == side))
    def _():
        out[...] = advance(advance(v[...], w, gains, odd, 0), w, gains, odd, 1)


def last_front_body(last, v, gains, w, kept, both):
    z, x, odd, half, second = where_am_i()
    both[1] = kept[...]

    @pl.when((z == last) & (half == 0))
    def _():
        both[0] = advance(advance(v[...], w, gains, odd, 0), w, gains, odd, 1)


def last_rear_body(last, got, kept, gains, w, out, corrected):
    z, x, odd, half, second = where_am_i()
    corrected[...] = kept[...] + got[1]

    @pl.when((z == last) & (half == 1))
    def _():
        out[...] = advance(advance(got[0], w, gains, odd, 0), w, gains, odd, 1)


def coarse_body(turn, far, near, offset, gains, w, kept_in, state_in, term, kept, state):
    z, x, odd, half, second = where_am_i()

    @pl.when(z == turn)
    def _():
        value = near[...] + far[...]
        state[...] = value
        held = jnp.where(half == 0, 1.0, 0.0).astype(F32)
        share = held * value + offset[...] + STEP * deltas(value, w, gains, odd, (0, 1))
        term[...] = share
        kept[...] = share


def final_body(start, handed, gains, w, state_0, state_1):
    z, x, odd, half, second = where_am_i()

    @pl.when(half == 0)
    def _():
        begin = jnp.where(z == 0, start[...], handed[...])
        after = advance(begin, w, gains, odd, 0)
        state_0[...] = after
        state_1[...] = advance(after, w, gains, odd, 1)


def pick_body(last, state_0, state_1, fresh, fresh_last, passed, gains, w, mine, send):
    z, x, odd, half, second = where_am_i()

    def put(even, uneven):
        mine[...] = jnp.where(odd == 0, even, uneven)
        send[...] = jnp.where(odd == 0, uneven, even)

    @pl.when(half == 0)
    def _():
        put(state_0[...], state_1[...])

    @pl.when(half == 1)
    def _():
        state = advance(passed[...], w, gains, odd, 0)
        put(state, jnp.where(z == last, fresh_last[...], fresh[...]))


def both_body(*refs):
    z, x, odd, half, second = where_am_i()
    for mine, got, out in zip(refs[0:4:2], refs[1:4:2], refs[4:], strict=True):
        out[second] = mine[...]
        out[1 - second] = got[...]


PARAMS = pltpu.CompilerParams(vmem_limit_bytes=12 * 2**20)
STATE = jax.ShapeDtypeStruct((FRAMES, WIDTH), F32)
PAIR = jax.ShapeDtypeStruct((2, FRAMES, WIDTH), F32)


def run(body, outs, *arrays, aliases=None, fixed=()):
    def kernel(*refs):
        body(*fixed, *refs)

    return pl.pallas_call(
        kernel,
        out_shape=outs,
        in_specs=[VMEM_SPEC] * len(arrays),
        out_specs=[VMEM_SPEC] * len(outs),
        input_output_aliases=aliases or {},
        compiler_params=PARAMS,
        name=body.__name__[:-5],
    )(*arrays)


def quarter():
    group = lax.axis_index("batch")
    return group // 2 % 2, group % 2


def own_piece(w, slot, base, chunk):
    parity, core = quarter()
    at = pl.multiple_of(base + (parity * 2 + core) * (chunk // 4), 32)
    return w[slot, pl.ds(at, chunk // 4), :].astype(F32)


def pack_body(attn_in, attn_out, mlp_in, mlp_out, norm_gain, head_gain, w, gains, *rest):
    outs, (norm, head, sem) = rest[:-3], rest[-3:]
    slot = where_am_i()[2]
    blocks = (
        [attn_in.at[0, :, pl.ds(i * WIDTH, WIDTH)] for i in range(3)]
        + [attn_out.at[0]]
        + [mlp_in.at[0, :, pl.ds(i * WIDTH, WIDTH)] for i in range(2)]
        + [mlp_out.at[0, pl.ds(i * WIDTH, WIDTH), :] for i in range(2)]
    )
    copies = [
        pltpu.make_async_copy(source, w.at[slot, pl.ds(i * WIDTH, WIDTH), :], sem.at[i])
        for i, source in enumerate(blocks)
    ] + [
        pltpu.make_async_copy(norm_gain, norm, sem.at[8]),
        pltpu.make_async_copy(head_gain, head, sem.at[9]),
    ]
    for copy in copies:
        copy.start()
    for copy in copies:
        copy.wait()
    tiled = jnp.concatenate([head[...]] * (WIDTH // HEAD), axis=1)
    gains[...] = jnp.concatenate([norm[...], tiled, jnp.zeros((6, WIDTH), F32)], axis=0)
    base = 0
    for chunk, out in zip(CHUNKS, outs, strict=True):
        out[: chunk // 4] = own_piece(w, slot, base, chunk)
        base += chunk
    outs[0][CHUNKS[0] // 4 :] = gains[...]


def pack(weights):
    return pl.pallas_call(
        pack_body,
        out_shape=[pltpu.VMEM((2, ROWS, WIDTH), BF16), jax.ShapeDtypeStruct((8, WIDTH), F32)]
        + [jax.ShapeDtypeStruct((rows, WIDTH), F32) for rows in PIECES],
        in_specs=[HBM_SPEC] * 6,
        out_specs=[VMEM_SPEC] * (2 + len(CHUNKS)),
        scratch_shapes=[
            pltpu.VMEM((1, WIDTH), F32),
            pltpu.VMEM((1, HEAD), F32),
            pltpu.SemaphoreType.DMA((10,)),
        ],
        compiler_params=PARAMS,
        name="pack",
    )(*weights)


def load_body(base, chunk, w_in, direct, beside, direct_swapped, beside_swapped, w):
    slot = 1 - where_am_i()[2]
    parity, core = quarter()
    for piece, number in (
        (direct, parity * 2 + core),
        (beside, (1 - parity) * 2 + core),
        (direct_swapped, parity * 2 + 1 - core),
        (beside_swapped, (1 - parity) * 2 + 1 - core),
    ):
        at = pl.multiple_of(base + number * (chunk // 4), 32)
        w[slot, pl.ds(at, chunk // 4), :] = piece[: chunk // 4].astype(BF16)


def load(base, chunk, w, *pieces):
    return run(
        load_body, [pltpu.VMEM((2, ROWS, WIDTH), BF16)], w, *pieces,
        aliases={0: 0}, fixed=(base, chunk),
    )[0]


def join_body(own, partner, out):
    out[...] = jnp.concatenate([own[...], partner[CHUNKS[0] // 4 :]], axis=0)


def on_device(inputs, attn_in, attn_out, mlp_in, mlp_out, norm_gain, head_gain):
    layers, groups = lax.axis_size("depth"), lax.axis_size("batch")
    blocks = layers // COARSEN
    last = blocks - 1
    everyone, front, rear = range(COARSEN), (0, 1), (2, 3)
    def move(array, pairs):
        return lax.ppermute(array, "depth", pairs)

    def within(array, source, by, low=0, high=blocks - 1):
        pairs = [
            (COARSEN * k + i, COARSEN * k + (i ^ by)) for k in range(low, high + 1) for i in source
        ]
        return move(array, pairs)

    weights = tuple(
        pltpu.with_memory_space_constraint(a, pltpu.HBM)
        for a in (attn_in, attn_out, mlp_in, mlp_out, norm_gain, head_gain)
    )
    w, own_gains, *packed = pack(weights)
    rows = groups // 2
    pairings = [
        [(2 * (r ^ 1) + c, 2 * r + c) for r in range(rows) for c in range(2)],
        [(2 * ((((r + 1) % rows) ^ 1) - 1) % groups + c, 2 * r + c) for r in range(rows) for c in range(2)],
    ]
    swap = [(g, g ^ 1) for g in range(groups)]
    base = 0
    for j, chunk in enumerate(CHUNKS):
        direct = within(packed[j], everyone, 1)
        if j == 0:
            (gains,) = run(join_body, [jax.ShapeDtypeStruct((16, WIDTH), F32)], own_gains, direct)
        beside = lax.ppermute(direct, "batch", pairings[j % 2])
        direct_swapped = lax.ppermute(direct, "batch", swap)
        beside_swapped = lax.ppermute(beside, "batch", swap)
        w = load(base, chunk, w, direct, beside, direct_swapped, beside_swapped)
        base += chunk

    moved, start = run(first_body, [STATE] * 2, inputs, gains, w)
    moved = within(moved, front, 3)
    (base,) = run(base_body, [STATE], start, gains, w)
    offset, term, kept = run(rest_body, [STATE] * 3, start, moved, base, gains, w)
    state = start
    for turn in range(1, blocks):
        pairs = [COARSEN * k + i for k in range((turn - 1) % 8, last, 8) for i in range(COARSEN)]
        far = move(term, [(p, (p ^ 3) + COARSEN) for p in pairs])
        near = move(term, [(p, p + COARSEN) for p in pairs])
        aliases = {5: 1, 6: 2} if turn < last else {5: 1}
        early = state
        term, kept, state = run(
            coarse_body, [STATE] * 3, far, near, offset, gains, w, kept, state,
            aliases=aliases, fixed=(turn,),
        )

    (middle,) = run(chain_body, [STATE], early, gains, w, fixed=(0, last - 1, 0))
    middle = within(middle, front, 3, 0, last - 1)
    (fresh,) = run(chain_body, [STATE], middle, gains, w, fixed=(0, last - 1, 1))
    handed = move(
        fresh, [(COARSEN * k + i, COARSEN * (k + 1) + (i ^ 3)) for k in range(last) for i in rear]
    )
    (shares,) = run(last_front_body, [PAIR], state, gains, w, kept, fixed=(last,))
    fresh_last, corrected = run(
        last_rear_body, [STATE] * 2, within(shares, everyone, 3), kept, gains, w, fixed=(last,)
    )
    state_0, state_1 = run(final_body, [STATE] * 2, start, handed, gains, w)
    mine, send = run(
        pick_body, [STATE] * 2, state_0, state_1, fresh, fresh_last,
        within(state_1, front, 3), gains, w, fixed=(last,),
    )

    output, ahead = run(
        both_body, [PAIR] * 2, mine, within(send, everyone, 1), corrected,
        within(corrected, everyone, 1),
    )
    return (output[None], ahead[None])


def solution(mesh):
    in_specs = (
        P("batch", None, None),
        P("depth", None, None),
        P("depth", None, None),
        P("depth", None, None),
        P("depth", None, None),
        P("depth", None),
        P("depth", None),
    )
    out_specs = (P("depth", "batch", None, None), P("depth", "batch", None, None))
    return jax.shard_map(
        on_device, mesh=mesh, in_specs=in_specs, out_specs=out_specs, check_vma=False
    )
```

```python
import jax
import jax.numpy as jnp
from jax import lax
from jax.experimental import pallas as pl
from jax.experimental.pallas import tpu as pltpu
from jax.sharding import PartitionSpec as P

F32, BF16 = jnp.float32, jnp.bfloat16
COARSEN = 4
STEP = 0.25
EPS = 1e-6
FRAMES, WIDTH, HEAD = 64, 512, 64
ROWS = 4096
CHUNKS = (1664, 1408, 1024)
PIECES = [chunk // 4 + (8 if j == 0 else 0) for j, chunk in enumerate(CHUNKS)]
QUAD = 4 * HEAD
VMEM_SPEC = pl.BlockSpec(memory_space=pltpu.VMEM)
HBM_SPEC = pl.BlockSpec(memory_space=pltpu.HBM)


def dot(left, right):
    return jnp.dot(left, right, preferred_element_type=F32)


def where_am_i():
    device = lax.axis_index("depth")
    x = device % COARSEN
    return device // COARSEN, x, x % 2, x // 2, x % 2 ^ x // 2


def gelu(up):
    return (0.5 * up * (1.0 + jnp.tanh(0.7978845608028654 * (up + 0.044715 * (up * up * up))))).astype(BF16)


def deltas(states, w, gains, layers, at):
    row = lax.broadcasted_iota(jnp.int32, (FRAMES, QUAD), 0)
    lane = lax.broadcasted_iota(jnp.int32, (FRAMES, QUAD), 1)
    causal = row >= lane % HEAD
    masks = [jnp.where(lane // HEAD == h, 1.0, 0.0).astype(BF16) for h in range(4)]
    ones = jnp.where(
        lax.broadcasted_iota(jnp.int32, (QUAD, QUAD), 0) // HEAD
        == lax.broadcasted_iota(jnp.int32, (QUAD, QUAD), 1) // HEAD,
        1.0,
        0.0,
    ).astype(BF16)
    each = range(len(layers))

    def block(n, i):
        return w[layers[n], i * WIDTH : (i + 1) * WIDTH, :]

    def rows(array, i):
        return array[i * FRAMES : (i + 1) * FRAMES]

    scaled = [v * lax.rsqrt(jnp.mean(v * v, axis=-1, keepdims=True) + EPS) for v in states]
    normed = [(scaled[n] * gains[pl.ds(at[n], 1), :]).astype(BF16) for n in each]
    stacked = []
    for n in each:
        both = [dot(normed[n], block(n, i)) for i in range(2)]
        stacked.append(jnp.concatenate([p[:, g : g + QUAD] for p in both for g in (0, QUAD)], axis=0))
    squares = [dot((s * s).astype(BF16), ones) * (1.0 / HEAD) for s in stacked]
    value = [dot(normed[n], block(n, 2)).astype(BF16) for n in each]
    up = [[dot(normed[n], block(n, 4 + i)) for i in range(2)] for n in each]
    exps, values = [], []
    for n in each:
        head_gain = gains[pl.ds(at[n] + 1, 1), :QUAD]
        unit = stacked[n] * lax.rsqrt(squares[n] + EPS) * head_gain
        for g in range(2):
            query = (rows(unit, g) * (HEAD**-0.5)).astype(BF16)
            key = rows(unit, 2 + g).astype(BF16)
            keys = jnp.concatenate([key * m for m in masks], axis=0)
            part = value[n][:, g * QUAD : (g + 1) * QUAD]
            values.append(jnp.concatenate([part * m for m in masks], axis=0))
            scores = lax.dot_general(
                query, keys, (((1,), (1,)), ((), ())), preferred_element_type=F32
            )
            exps.append(jnp.where(causal, jnp.exp(scores), 0.0).astype(BF16))
    hidden = [[gelu(u) for u in up[n]] for n in each]
    down = [dot(hidden[n][0], block(n, 6)) + dot(hidden[n][1], block(n, 7)) for n in each]
    sums = dot(jnp.concatenate(exps, axis=0), ones)
    for n in each:
        context = jnp.concatenate(
            [dot(exps[i], values[i]) / rows(sums, i) for i in (2 * n, 2 * n + 1)], axis=1
        ).astype(BF16)
        down[n] = down[n] + dot(context, block(n, 3))
    return down


def advance(v, w, gains, odd, layer):
    return v + STEP * deltas([v], w, gains, [layer], [(odd + layer) % 2 * 8])[0]


def pair_sum(v, w, gains, odd):
    one, two = deltas([v, v], w, gains, [0, 1], [odd * 8, (odd + 1) % 2 * 8])
    return one + two


def own_body(position, v, gains, w_in, w, moved):
    z, x, odd, half, second = where_am_i()

    @pl.when(x == position)
    def _():
        states = [v[0], v[1]]
        changes = deltas(states, w, gains, [odd, odd], [0, 0])
        for i in range(2):
            moved[i] = states[i] + STEP * changes[i]


def ended_body(inputs, ended, got, term, kept, state):
    z, x, odd, half, second = where_am_i()
    state[...] = inputs[second]
    value = jnp.where(half == 0, 0.0, jnp.where(odd == 0, got[...], ended[second]))
    term[...] = value
    kept[...] = value


def offset_body(state, kept, gains, w, offset):
    z, x, odd, half, second = where_am_i()
    start = state[...]
    change = jnp.where(half == 0, 0.0, kept[...] - start)
    offset[...] = change - STEP * pair_sum(start, w, gains, odd)


def chain_body(low, high, side, v, gains, w, out):
    z, x, odd, half, second = where_am_i()

    @pl.when((z >= low) & (z <= high) & (half == side))
    def _():
        out[...] = advance(advance(v[...], w, gains, odd, 0), w, gains, odd, 1)


def last_front_body(last, v, gains, w, kept, both):
    z, x, odd, half, second = where_am_i()
    both[1] = kept[...]

    @pl.when((z == last) & (half == 0))
    def _():
        both[0] = advance(advance(v[...], w, gains, odd, 0), w, gains, odd, 1)


def last_rear_body(last, got, kept, gains, w, out, corrected):
    z, x, odd, half, second = where_am_i()
    corrected[...] = kept[...] + got[1]

    @pl.when((z == last) & (half == 1))
    def _():
        out[...] = advance(advance(got[0], w, gains, odd, 0), w, gains, odd, 1)


def coarse_body(turn, far, near, offset, gains, w, kept_in, state_in, term, kept, state):
    z, x, odd, half, second = where_am_i()

    @pl.when(z == turn)
    def _():
        value = near[...] + far[...]
        state[...] = value
        held = jnp.where(half == 0, 1.0, 0.0).astype(F32)
        share = held * value + offset[...] + STEP * pair_sum(value, w, gains, odd)
        term[...] = share
        kept[...] = share


def final_body(start, handed, gains, w, state_0, state_1):
    z, x, odd, half, second = where_am_i()

    @pl.when(half == 0)
    def _():
        begin = jnp.where(z == 0, start[...], handed[...])
        after = advance(begin, w, gains, odd, 0)
        state_0[...] = after
        state_1[...] = advance(after, w, gains, odd, 1)


def pick_body(last, state_0, state_1, fresh, fresh_last, passed, gains, w, mine, send):
    z, x, odd, half, second = where_am_i()

    def put(even, uneven):
        mine[...] = jnp.where(odd == 0, even, uneven)
        send[...] = jnp.where(odd == 0, uneven, even)

    @pl.when(half == 0)
    def _():
        put(state_0[...], state_1[...])

    @pl.when(half == 1)
    def _():
        state = advance(passed[...], w, gains, odd, 0)
        put(state, jnp.where(z == last, fresh_last[...], fresh[...]))


def both_body(*refs):
    z, x, odd, half, second = where_am_i()
    for mine, got, out in zip(refs[0:4:2], refs[1:4:2], refs[4:], strict=True):
        out[second] = mine[...]
        out[1 - second] = got[...]


PARAMS = pltpu.CompilerParams(vmem_limit_bytes=12 * 2**20)
STATE = jax.ShapeDtypeStruct((FRAMES, WIDTH), F32)
PAIR = jax.ShapeDtypeStruct((2, FRAMES, WIDTH), F32)


def run(body, outs, *arrays, aliases=None, fixed=()):
    def kernel(*refs):
        body(*fixed, *refs)

    return pl.pallas_call(
        kernel,
        out_shape=outs,
        in_specs=[VMEM_SPEC] * len(arrays),
        out_specs=[VMEM_SPEC] * len(outs),
        input_output_aliases=aliases or {},
        compiler_params=PARAMS,
        name=body.__name__[:-5],
    )(*arrays)


def quarter():
    group = lax.axis_index("batch")
    return group // 2 % 2, group % 2


def own_piece(w, slot, base, chunk):
    parity, core = quarter()
    at = pl.multiple_of(base + (parity * 2 + core) * (chunk // 4), 32)
    return w[slot, pl.ds(at, chunk // 4), :].astype(F32)


def pack_body(attn_in, attn_out, mlp_in, mlp_out, norm_gain, head_gain, w, gains, *rest):
    outs, (norm, head, sem) = rest[:-3], rest[-3:]
    slot = where_am_i()[2]
    blocks = (
        [attn_in.at[0, :, pl.ds(i * WIDTH, WIDTH)] for i in range(3)]
        + [attn_out.at[0]]
        + [mlp_in.at[0, :, pl.ds(i * WIDTH, WIDTH)] for i in range(2)]
        + [mlp_out.at[0, pl.ds(i * WIDTH, WIDTH), :] for i in range(2)]
    )
    copies = [
        pltpu.make_async_copy(source, w.at[slot, pl.ds(i * WIDTH, WIDTH), :], sem.at[i])
        for i, source in enumerate(blocks)
    ] + [
        pltpu.make_async_copy(norm_gain, norm, sem.at[8]),
        pltpu.make_async_copy(head_gain, head, sem.at[9]),
    ]
    for copy in copies:
        copy.start()
    for copy in copies:
        copy.wait()
    tiled = jnp.concatenate([head[...]] * (WIDTH // HEAD), axis=1)
    gains[...] = jnp.concatenate([norm[...], tiled, jnp.zeros((6, WIDTH), F32)], axis=0)
    base = 0
    for chunk, out in zip(CHUNKS, outs, strict=True):
        out[: chunk // 4] = own_piece(w, slot, base, chunk)
        base += chunk
    outs[0][CHUNKS[0] // 4 :] = gains[...]


def pack(weights):
    return pl.pallas_call(
        pack_body,
        out_shape=[pltpu.VMEM((2, ROWS, WIDTH), BF16), jax.ShapeDtypeStruct((8, WIDTH), F32)]
        + [jax.ShapeDtypeStruct((rows, WIDTH), F32) for rows in PIECES],
        in_specs=[HBM_SPEC] * 6,
        out_specs=[VMEM_SPEC] * (2 + len(CHUNKS)),
        scratch_shapes=[
            pltpu.VMEM((1, WIDTH), F32),
            pltpu.VMEM((1, HEAD), F32),
            pltpu.SemaphoreType.DMA((10,)),
        ],
        compiler_params=PARAMS,
        name="pack",
    )(*weights)


def load_body(base, chunk, w_in, direct, beside, direct_swapped, beside_swapped, w):
    slot = 1 - where_am_i()[2]
    parity, core = quarter()
    for piece, number in (
        (direct, parity * 2 + core),
        (beside, (1 - parity) * 2 + core),
        (direct_swapped, parity * 2 + 1 - core),
        (beside_swapped, (1 - parity) * 2 + 1 - core),
    ):
        at = pl.multiple_of(base + number * (chunk // 4), 32)
        w[slot, pl.ds(at, chunk // 4), :] = piece[: chunk // 4].astype(BF16)


def load(base, chunk, w, *pieces):
    return run(
        load_body, [pltpu.VMEM((2, ROWS, WIDTH), BF16)], w, *pieces,
        aliases={0: 0}, fixed=(base, chunk),
    )[0]


def join_body(own, partner, out):
    out[...] = jnp.concatenate([own[...], partner[CHUNKS[0] // 4 :]], axis=0)


def on_device(inputs, attn_in, attn_out, mlp_in, mlp_out, norm_gain, head_gain):
    layers, groups = lax.axis_size("depth"), lax.axis_size("batch")
    blocks = layers // COARSEN
    last = blocks - 1
    everyone, front, rear = range(COARSEN), (0, 1), (2, 3)
    def move(array, pairs):
        return lax.ppermute(array, "depth", pairs)

    def within(array, source, by, low=0, high=blocks - 1):
        pairs = [
            (COARSEN * k + i, COARSEN * k + (i ^ by)) for k in range(low, high + 1) for i in source
        ]
        return move(array, pairs)

    weights = tuple(
        pltpu.with_memory_space_constraint(a, pltpu.HBM)
        for a in (attn_in, attn_out, mlp_in, mlp_out, norm_gain, head_gain)
    )
    w, own_gains, *packed = pack(weights)
    rows = groups // 2
    pairings = [
        [(2 * (r ^ 1) + c, 2 * r + c) for r in range(rows) for c in range(2)],
        [(2 * ((((r + 1) % rows) ^ 1) - 1) % groups + c, 2 * r + c) for r in range(rows) for c in range(2)],
    ]
    swap = [(g, g ^ 1) for g in range(groups)]
    moved = inputs
    for position in range(COARSEN):
        w, moved = run(
            own_body, [pltpu.VMEM((2, ROWS, WIDTH), BF16), PAIR], moved, own_gains, w,
            aliases={2: 0}, fixed=(position,),
        )
        if position < COARSEN - 1:
            moved = within(moved, (position,), position ^ (position + 1))
    got = within(moved[1], (3,), 1)
    term, kept, start = run(ended_body, [STATE] * 3, inputs, moved, got)
    base = 0
    for j, chunk in enumerate(CHUNKS):
        direct = within(packed[j], everyone, 1)
        if j == 0:
            (gains,) = run(join_body, [jax.ShapeDtypeStruct((16, WIDTH), F32)], own_gains, direct)
        beside = lax.ppermute(direct, "batch", pairings[j % 2])
        direct_swapped = lax.ppermute(direct, "batch", swap)
        beside_swapped = lax.ppermute(beside, "batch", swap)
        w = load(base, chunk, w, direct, beside, direct_swapped, beside_swapped)
        base += chunk

    (offset,) = run(offset_body, [STATE], start, kept, gains, w)
    state = start
    for turn in range(1, blocks):
        pairs = [COARSEN * k + i for k in range((turn - 1) % 8, last, 8) for i in range(COARSEN)]
        far = move(term, [(p, (p ^ 3) + COARSEN) for p in pairs])
        near = move(term, [(p, p + COARSEN) for p in pairs])
        aliases = {5: 1, 6: 2} if turn < last else {5: 1}
        early = state
        term, kept, state = run(
            coarse_body, [STATE] * 3, far, near, offset, gains, w, kept, state,
            aliases=aliases, fixed=(turn,),
        )

    (middle,) = run(chain_body, [STATE], early, gains, w, fixed=(0, last - 1, 0))
    middle = within(middle, front, 3, 0, last - 1)
    (fresh,) = run(chain_body, [STATE], middle, gains, w, fixed=(0, last - 1, 1))
    handed = move(
        fresh, [(COARSEN * k + i, COARSEN * (k + 1) + (i ^ 3)) for k in range(last) for i in rear]
    )
    (shares,) = run(last_front_body, [PAIR], state, gains, w, kept, fixed=(last,))
    fresh_last, corrected = run(
        last_rear_body, [STATE] * 2, within(shares, everyone, 3), kept, gains, w, fixed=(last,)
    )
    state_0, state_1 = run(final_body, [STATE] * 2, start, handed, gains, w)
    mine, send = run(
        pick_body, [STATE] * 2, state_0, state_1, fresh, fresh_last,
        within(state_1, front, 3), gains, w, fixed=(last,),
    )

    output, ahead = run(
        both_body, [PAIR] * 2, mine, within(send, everyone, 1), corrected,
        within(corrected, everyone, 1),
    )
    return (output[None], ahead[None])


def solution(mesh):
    in_specs = (
        P("batch", None, None),
        P("depth", None, None),
        P("depth", None, None),
        P("depth", None, None),
        P("depth", None, None),
        P("depth", None),
        P("depth", None),
    )
    out_specs = (P("depth", "batch", None, None), P("depth", "batch", None, None))
    return jax.shard_map(
        on_device, mesh=mesh, in_specs=in_specs, out_specs=out_specs, check_vma=False
    )
```

```python
import jax
import jax.numpy as jnp
from jax import lax
from jax.experimental import pallas as pl
from jax.experimental.pallas import tpu as pltpu
from jax.sharding import PartitionSpec as P

F32, BF16 = jnp.float32, jnp.bfloat16
COARSEN = 4
STEP = 0.25
EPS = 1e-6
FRAMES, WIDTH, HEAD = 64, 512, 64
ROWS = 4096
CHUNKS = (1664, 1408, 1024)
PIECES = [chunk // 4 + (8 if j == 0 else 0) for j, chunk in enumerate(CHUNKS)]
QUAD = 4 * HEAD
VMEM_SPEC = pl.BlockSpec(memory_space=pltpu.VMEM)
HBM_SPEC = pl.BlockSpec(memory_space=pltpu.HBM)


def dot(left, right):
    return jnp.dot(left, right, preferred_element_type=F32)


def where_am_i():
    device = lax.axis_index("depth")
    x = device % COARSEN
    return device // COARSEN, x, x % 2, x // 2, x % 2 ^ x // 2


def gelu(up):
    return (0.5 * up * (1.0 + jnp.tanh(0.7978845608028654 * (up + 0.044715 * (up * up * up))))).astype(BF16)


def deltas(v, w, gains, odd, layers):
    row = lax.broadcasted_iota(jnp.int32, (FRAMES, QUAD), 0)
    lane = lax.broadcasted_iota(jnp.int32, (FRAMES, QUAD), 1)
    causal = row >= lane % HEAD
    masks = [jnp.where(lane // HEAD == h, 1.0, 0.0).astype(BF16) for h in range(4)]
    ones = jnp.where(
        lax.broadcasted_iota(jnp.int32, (QUAD, QUAD), 0) // HEAD
        == lax.broadcasted_iota(jnp.int32, (QUAD, QUAD), 1) // HEAD,
        1.0,
        0.0,
    ).astype(BF16)
    each = range(len(layers))

    def block(n, i):
        return w[layers[n], i * WIDTH : (i + 1) * WIDTH, :]

    def rows(array, i):
        return array[i * FRAMES : (i + 1) * FRAMES]

    at = [(odd + layer) % 2 * 8 for layer in layers]
    scaled = v * lax.rsqrt(jnp.mean(v * v, axis=-1, keepdims=True) + EPS)
    normed = [(scaled * gains[pl.ds(at[n], 1), :]).astype(BF16) for n in each]
    stacked = []
    for n in each:
        both = [dot(normed[n], block(n, i)) for i in range(2)]
        stacked.append(jnp.concatenate([p[:, g : g + QUAD] for p in both for g in (0, QUAD)], axis=0))
    squares = [dot((s * s).astype(BF16), ones) * (1.0 / HEAD) for s in stacked]
    value = [dot(normed[n], block(n, 2)).astype(BF16) for n in each]
    up = [[dot(normed[n], block(n, 4 + i)) for i in range(2)] for n in each]
    exps, values = [], []
    for n in each:
        head_gain = gains[pl.ds(at[n] + 1, 1), :QUAD]
        unit = stacked[n] * lax.rsqrt(squares[n] + EPS) * head_gain
        for g in range(2):
            query = (rows(unit, g) * (HEAD**-0.5)).astype(BF16)
            key = rows(unit, 2 + g).astype(BF16)
            keys = jnp.concatenate([key * m for m in masks], axis=0)
            part = value[n][:, g * QUAD : (g + 1) * QUAD]
            values.append(jnp.concatenate([part * m for m in masks], axis=0))
            scores = lax.dot_general(
                query, keys, (((1,), (1,)), ((), ())), preferred_element_type=F32
            )
            exps.append(jnp.where(causal, jnp.exp(scores), 0.0).astype(BF16))
    hidden = [[gelu(u) for u in up[n]] for n in each]
    down = [dot(hidden[n][0], block(n, 6)) + dot(hidden[n][1], block(n, 7)) for n in each]
    sums = dot(jnp.concatenate(exps, axis=0), ones)
    for n in each:
        context = jnp.concatenate(
            [dot(exps[i], values[i]) / rows(sums, i) for i in (2 * n, 2 * n + 1)], axis=1
        ).astype(BF16)
        down[n] = down[n] + dot(context, block(n, 3))
    return down


def advance(v, w, gains, odd, layer):
    return v + STEP * deltas(v, w, gains, odd, (layer,))[0]


def first_body(inputs, gains, w, moved, state):
    z, x, odd, half, second = where_am_i()
    start = inputs[second]
    state[...] = start

    @pl.when(half == 0)
    def _():
        moved[...] = advance(advance(start, w, gains, odd, 0), w, gains, odd, 1)


def base_body(state, gains, w, base):
    z, x, odd, half, second = where_am_i()
    one, two = deltas(state[...], w, gains, odd, (0, 1))
    base[...] = STEP * (one + two)


def rest_body(start, moved, base, gains, w, offset, term, kept):
    z, x, odd, half, second = where_am_i()

    @pl.when(half == 0)
    def _():
        offset[...] = -base[...]
        term[...] = jnp.zeros_like(term)
        kept[...] = jnp.zeros_like(kept)

    @pl.when(half == 1)
    def _():
        state = advance(advance(moved[...], w, gains, odd, 0), w, gains, odd, 1)
        offset[...] = state - start[...] - base[...]
        term[...] = state
        kept[...] = state


def chain_body(low, high, side, v, gains, w, out):
    z, x, odd, half, second = where_am_i()

    @pl.when((z >= low) & (z <= high) & (half == side))
    def _():
        out[...] = advance(advance(v[...], w, gains, odd, 0), w, gains, odd, 1)


def last_front_body(last, v, gains, w, kept, both):
    z, x, odd, half, second = where_am_i()
    both[1] = kept[...]

    @pl.when((z == last) & (half == 0))
    def _():
        both[0] = advance(advance(v[...], w, gains, odd, 0), w, gains, odd, 1)


def last_rear_body(last, got, kept, gains, w, out, corrected):
    z, x, odd, half, second = where_am_i()
    corrected[...] = kept[...] + got[1]

    @pl.when((z == last) & (half == 1))
    def _():
        out[...] = advance(advance(got[0], w, gains, odd, 0), w, gains, odd, 1)


def coarse_body(turn, far, near, offset, gains, w, kept_in, state_in, *outs):
    kept, state, *term = outs[:3]
    middle = outs[3:]
    z, x, odd, half, second = where_am_i()

    @pl.when(z == turn)
    def _():
        value = near[...] + far[...]
        state[...] = value
        held = jnp.where(half == 0, 1.0, 0.0).astype(F32)
        one, two = deltas(value, w, gains, odd, (0, 1))
        share = held * value + offset[...] + STEP * (one + two)
        for out in (*term, kept):
            out[...] = share
        for out in middle:

            @pl.when(half == 0)
            def _():
                out[...] = advance(value + STEP * one, w, gains, odd, 1)

    for out in middle:

        @pl.when((z < turn) & (half == 0))
        def _():
            out[...] = advance(advance(state_in[...], w, gains, odd, 0), w, gains, odd, 1)


def final_body(start, handed, gains, w, state_0, state_1):
    z, x, odd, half, second = where_am_i()

    @pl.when(half == 0)
    def _():
        begin = jnp.where(z == 0, start[...], handed[...])
        after = advance(begin, w, gains, odd, 0)
        state_0[...] = after
        state_1[...] = advance(after, w, gains, odd, 1)


def pick_body(last, state_0, state_1, fresh, fresh_last, passed, gains, w, mine, send):
    z, x, odd, half, second = where_am_i()

    def put(even, uneven):
        mine[...] = jnp.where(odd == 0, even, uneven)
        send[...] = jnp.where(odd == 0, uneven, even)

    @pl.when(half == 0)
    def _():
        put(state_0[...], state_1[...])

    @pl.when(half == 1)
    def _():
        state = advance(passed[...], w, gains, odd, 0)
        put(state, jnp.where(z == last, fresh_last[...], fresh[...]))


def both_body(*refs):
    z, x, odd, half, second = where_am_i()
    for mine, got, out in zip(refs[0:4:2], refs[1:4:2], refs[4:], strict=True):
        out[second] = mine[...]
        out[1 - second] = got[...]


PARAMS = pltpu.CompilerParams(vmem_limit_bytes=12 * 2**20)
STATE = jax.ShapeDtypeStruct((FRAMES, WIDTH), F32)
PAIR = jax.ShapeDtypeStruct((2, FRAMES, WIDTH), F32)


def run(body, outs, *arrays, aliases=None, fixed=()):
    def kernel(*refs):
        body(*fixed, *refs)

    return pl.pallas_call(
        kernel,
        out_shape=outs,
        in_specs=[VMEM_SPEC] * len(arrays),
        out_specs=[VMEM_SPEC] * len(outs),
        input_output_aliases=aliases or {},
        compiler_params=PARAMS,
        name=body.__name__[:-5],
    )(*arrays)


def quarter():
    group = lax.axis_index("batch")
    return group // 2 % 2, group % 2


def own_piece(w, slot, base, chunk):
    parity, core = quarter()
    at = pl.multiple_of(base + (parity * 2 + core) * (chunk // 4), 32)
    return w[slot, pl.ds(at, chunk // 4), :].astype(F32)


def pack_body(attn_in, attn_out, mlp_in, mlp_out, norm_gain, head_gain, w, gains, *rest):
    outs, (norm, head, sem) = rest[:-3], rest[-3:]
    slot = where_am_i()[2]
    blocks = (
        [attn_in.at[0, :, pl.ds(i * WIDTH, WIDTH)] for i in range(3)]
        + [attn_out.at[0]]
        + [mlp_in.at[0, :, pl.ds(i * WIDTH, WIDTH)] for i in range(2)]
        + [mlp_out.at[0, pl.ds(i * WIDTH, WIDTH), :] for i in range(2)]
    )
    copies = [
        pltpu.make_async_copy(source, w.at[slot, pl.ds(i * WIDTH, WIDTH), :], sem.at[i])
        for i, source in enumerate(blocks)
    ] + [
        pltpu.make_async_copy(norm_gain, norm, sem.at[8]),
        pltpu.make_async_copy(head_gain, head, sem.at[9]),
    ]
    for copy in copies:
        copy.start()
    for copy in copies:
        copy.wait()
    tiled = jnp.concatenate([head[...]] * (WIDTH // HEAD), axis=1)
    gains[...] = jnp.concatenate([norm[...], tiled, jnp.zeros((6, WIDTH), F32)], axis=0)
    base = 0
    for chunk, out in zip(CHUNKS, outs, strict=True):
        out[: chunk // 4] = own_piece(w, slot, base, chunk)
        base += chunk
    outs[0][CHUNKS[0] // 4 :] = gains[...]


def pack(weights):
    return pl.pallas_call(
        pack_body,
        out_shape=[pltpu.VMEM((2, ROWS, WIDTH), BF16), jax.ShapeDtypeStruct((8, WIDTH), F32)]
        + [jax.ShapeDtypeStruct((rows, WIDTH), F32) for rows in PIECES],
        in_specs=[HBM_SPEC] * 6,
        out_specs=[VMEM_SPEC] * (2 + len(CHUNKS)),
        scratch_shapes=[
            pltpu.VMEM((1, WIDTH), F32),
            pltpu.VMEM((1, HEAD), F32),
            pltpu.SemaphoreType.DMA((10,)),
        ],
        compiler_params=PARAMS,
        name="pack",
    )(*weights)


def load_body(base, chunk, w_in, direct, beside, direct_swapped, beside_swapped, w):
    slot = 1 - where_am_i()[2]
    parity, core = quarter()
    for piece, number in (
        (direct, parity * 2 + core),
        (beside, (1 - parity) * 2 + core),
        (direct_swapped, parity * 2 + 1 - core),
        (beside_swapped, (1 - parity) * 2 + 1 - core),
    ):
        at = pl.multiple_of(base + number * (chunk // 4), 32)
        w[slot, pl.ds(at, chunk // 4), :] = piece[: chunk // 4].astype(BF16)


def load(base, chunk, w, *pieces):
    return run(
        load_body, [pltpu.VMEM((2, ROWS, WIDTH), BF16)], w, *pieces,
        aliases={0: 0}, fixed=(base, chunk),
    )[0]


def join_body(own, partner, out):
    out[...] = jnp.concatenate([own[...], partner[CHUNKS[0] // 4 :]], axis=0)


def on_device(inputs, attn_in, attn_out, mlp_in, mlp_out, norm_gain, head_gain):
    layers, groups = lax.axis_size("depth"), lax.axis_size("batch")
    blocks = layers // COARSEN
    last = blocks - 1
    everyone, front, rear = range(COARSEN), (0, 1), (2, 3)
    def move(array, pairs):
        return lax.ppermute(array, "depth", pairs)

    def within(array, source, by, low=0, high=blocks - 1):
        pairs = [
            (COARSEN * k + i, COARSEN * k + (i ^ by)) for k in range(low, high + 1) for i in source
        ]
        return move(array, pairs)

    weights = tuple(
        pltpu.with_memory_space_constraint(a, pltpu.HBM)
        for a in (attn_in, attn_out, mlp_in, mlp_out, norm_gain, head_gain)
    )
    w, own_gains, *packed = pack(weights)
    rows = groups // 2
    pairings = [
        [(2 * (r ^ 1) + c, 2 * r + c) for r in range(rows) for c in range(2)],
        [(2 * ((((r + 1) % rows) ^ 1) - 1) % groups + c, 2 * r + c) for r in range(rows) for c in range(2)],
    ]
    swap = [(g, g ^ 1) for g in range(groups)]
    base = 0
    for j, chunk in enumerate(CHUNKS):
        direct = within(packed[j], everyone, 1)
        if j == 0:
            (gains,) = run(join_body, [jax.ShapeDtypeStruct((16, WIDTH), F32)], own_gains, direct)
        beside = lax.ppermute(direct, "batch", pairings[j % 2])
        direct_swapped = lax.ppermute(direct, "batch", swap)
        beside_swapped = lax.ppermute(beside, "batch", swap)
        w = load(base, chunk, w, direct, beside, direct_swapped, beside_swapped)
        base += chunk

    moved, start = run(first_body, [STATE] * 2, inputs, gains, w)
    moved = within(moved, front, 3)
    (base,) = run(base_body, [STATE], start, gains, w)
    offset, term, kept = run(rest_body, [STATE] * 3, start, moved, base, gains, w)
    state = start
    for turn in range(1, blocks):
        pairs = [COARSEN * k + i for k in range((turn - 1) % 8, last, 8) for i in range(COARSEN)]
        far = move(term, [(p, (p ^ 3) + COARSEN) for p in pairs])
        near = move(term, [(p, p + COARSEN) for p in pairs])
        count = {last - 1: 4, last: 2}.get(turn, 3)
        kept, state, *more = run(
            coarse_body, [STATE] * count, far, near, offset, gains, w, kept, state,
            aliases={5: 0, 6: 1}, fixed=(turn,),
        )
        if turn < last:
            term = more[0]
        if turn == last - 1:
            middle = more[1]

    middle = within(middle, front, 3, 0, last - 1)
    (fresh,) = run(chain_body, [STATE], middle, gains, w, fixed=(0, last - 1, 1))
    handed = move(
        fresh, [(COARSEN * k + i, COARSEN * (k + 1) + (i ^ 3)) for k in range(last) for i in rear]
    )
    (shares,) = run(last_front_body, [PAIR], state, gains, w, kept, fixed=(last,))
    fresh_last, corrected = run(
        last_rear_body, [STATE] * 2, within(shares, everyone, 3), kept, gains, w, fixed=(last,)
    )
    state_0, state_1 = run(final_body, [STATE] * 2, start, handed, gains, w)
    mine, send = run(
        pick_body, [STATE] * 2, state_0, state_1, fresh, fresh_last,
        within(state_1, front, 3), gains, w, fixed=(last,),
    )

    output, ahead = run(
        both_body, [PAIR] * 2, mine, within(send, everyone, 1), corrected,
        within(corrected, everyone, 1),
    )
    return (output[None], ahead[None])


def solution(mesh):
    in_specs = (
        P("batch", None, None),
        P("depth", None, None),
        P("depth", None, None),
        P("depth", None, None),
        P("depth", None, None),
        P("depth", None),
        P("depth", None),
    )
    out_specs = (P("depth", "batch", None, None), P("depth", "batch", None, None))
    return jax.shard_map(
        on_device, mesh=mesh, in_specs=in_specs, out_specs=out_specs, check_vma=False
    )
```
